256 devices in a mesh: node: 64 (over x_hi, z, y), head: 4 (over x_lo, core).
Axes of the slice: x: 4 (x_hi: 2, x_lo: 2; x = x_hi * 2 + x_lo), y: 4, z: 8, core: 2. Of those that a mesh axis runs over, the one named last changes fastest.
Arguments:
- queries: bfloat16 [16384, 8192], P('node', 'head'), may hold values from -15 to 15
- own_cache: bfloat16 [2, 16384, 1024], P(None, 'node', 'head'), may hold values from -12 to 12
- tree_cache: bfloat16 [2, 65536, 1024], P(None, 'node', 'head'), may hold values from -6 to 6
- shared_cache: bfloat16 [2, 512, 1024], P(None, None, 'head'), may hold values from -6 to 6
- parent: int32 [128], replicated, may hold values from -1 to 127, as said below
- leaf: int32 [128], P('node'), may hold values from 0 to 127, as said below
Outputs:
- attended: bfloat16 [16384, 8192], P(('node', 'head'))
The draws below stay inside these ranges and needn't reach their ends.
Inputs may be any that keep to these rules, and one draw needn't show every extreme that they name: The 128 tree blocks fall into runs of 8 consecutive blocks, counted cyclically (block 127 is followed by block 0); each run is one subtree: its first block has parent -1 and every other block's parent is an earlier block of the same run. Every path thus holds at most 8 blocks. Branch b hangs under a block of its own node: leaf[b] // 2 == b // 2, where block i lies on node i // 2. Every block on the path of a branch of node n lies on one of the nodes n - 4 to n, counted modulo 128 / 2. Some branch's path holds exactly 8 blocks and reaches node n - 4.
All inputs are finite; a program needn't handle non-finite values.
Results may differ from the reference program's by a relative error of at most 0.011.
Values may be sent and summed in bfloat16 or wider, within the bound.
A program may use at most 128 MiB of HBM per device.

```python
import math
import jax
import jax.numpy as jnp
from jax import lax

QH = 64
KVH = 8
HD = 128
BT = 512
BQ = 128
SUB = 8
BLK_DEV = 2
BR_DEV = 2
NBLK = 128
BRANCHES = 128
QROWS = 16384
KROWS = 65536


def tree_layout(key):
    base = jax.random.fold_in(key, 5)
    first, second = jax.random.split(base)
    offset = BLK_DEV * jax.random.randint(first, (), 0, NBLK // BLK_DEV) + (1 - SUB) % BLK_DEV
    chosen = jax.random.randint(second, (), 0, NBLK // SUB)
    return (offset, chosen)


def draw_parent(key, part):
    offset, chosen = tree_layout(key)
    key = jax.random.fold_in(key, 31)
    index = jnp.arange(NBLK, dtype=jnp.int32)
    shifted = (index - offset) % NBLK
    inner = shifted % SUB
    run = shifted // SUB
    pick = jax.random.randint(key, (NBLK,), 0, jnp.maximum(inner, 1))
    earlier = jnp.where(run == chosen, inner - 1, pick)
    return jnp.where(inner == 0, -1, (offset + run * SUB + earlier) % NBLK).astype(jnp.int32)


def draw_leaf(key, part):
    offset, chosen = tree_layout(key)
    key = jax.random.fold_in(key, 37)
    branch = jnp.arange(BRANCHES, dtype=jnp.int32)
    owner = branch // BR_DEV
    pick = jax.random.randint(key, (BRANCHES,), 0, BLK_DEV)
    deepest = (offset + chosen * SUB + SUB - 1) % NBLK
    target = deepest // BLK_DEV
    fixed = (owner == target) & (branch % BR_DEV == 0)
    return jnp.where(fixed, deepest, owner * BLK_DEV + pick).astype(jnp.int32)


def draw_queries(key, part):
    key = jax.random.fold_in(key, 41)
    drawn = jnp.clip(2.5 * jax.random.normal(key, (QROWS, QH * HD)), -15.0, 15.0)
    return drawn.astype(jnp.bfloat16)


def draw_own_cache(key, part):
    key = jax.random.fold_in(key, 43)
    first, second = jax.random.split(key)
    keys = jnp.clip(jax.random.normal(first, (QROWS, KVH * HD)), -6.0, 6.0)
    values = jnp.clip(jax.random.normal(second, (QROWS, KVH * HD)), -6.0, 6.0)
    return jnp.stack([keys, values]).astype(jnp.bfloat16)


def block_scale(stream_key, shape, pieces, smallest, high):
    def one(axis_at, blocks):
        steps = jax.random.uniform(jax.random.fold_in(jax.random.fold_in(stream_key, 6), axis_at), (blocks,), jnp.float32, smallest / len(pieces), high / len(pieces))
        return jnp.repeat(jnp.exp(steps), shape[axis_at] // blocks).reshape((-1,) + (1,) * (len(shape) - axis_at - 1))

    level = one(*pieces[0])
    for cut in pieces[1:]:
        level = level * one(*cut)
    return level


def normal_values(own_key, extent, scale, reach, pieces=(), kind=jnp.bfloat16):
    values = jax.random.normal(own_key, extent, jnp.float32) * scale
    if len(pieces) > 0:
        values = block_scale(own_key, extent, pieces, -0.22, 0.18) * values
    return jnp.clip(values, min=-reach, max=reach).astype(kind)


def setup_inputs(seed: int = 0) -> dict:
    streams_of = jax.random.split(jax.random.key(seed), 7)
    return {
        "queries": draw_queries(jax.random.fold_in(streams_of[6], 71), 0),
        "own_cache": draw_own_cache(jax.random.fold_in(streams_of[6], 71), 0),
        "tree_cache": normal_values(streams_of[2], (2, KROWS, KVH * HD), 1.0, 6.0, ((1, 64), (2, 4))),
        "shared_cache": normal_values(streams_of[3], (2, BT, KVH * HD), 1.0, 6.0, ((2, 4),)),
        "parent": draw_parent(jax.random.fold_in(streams_of[6], 71), 0),
        "leaf": draw_leaf(jax.random.fold_in(streams_of[6], 71), 0),
    }


BASE = 1000000.0
NEG = -1e+30

def rotate(field, where_at):
    half = HD // 2
    inverse = jnp.power(jnp.float32(BASE), -jnp.arange(half).astype(jnp.float32) * (2.0 / HD))
    angle = where_at.astype(jnp.float32)[:, None] * inverse[None, :]
    cosine = jnp.cos(angle)[:, None, :]
    sine = jnp.sin(angle)[:, None, :]
    first = field[..., :half]
    second = field[..., half:]
    return jnp.concatenate([first * cosine - second * sine, second * cosine + first * sine], axis=-1)

def path_of(leaf_ids, parent):
    chain = []
    current = leaf_ids
    for step in range(SUB):
        chain.append(current)
        current = jnp.where(current >= 0, parent[jnp.maximum(current, 0)], -1).astype(jnp.int32)
    return jnp.stack(chain, axis=-1)

def block_terms(query_block, keys, values, valid, mask):
    count = keys.shape[0]
    key_heads = keys.reshape(count, -1, HD).astype(jnp.float32)
    value_heads = values.reshape(count, -1, HD).astype(jnp.float32)
    scores = jnp.einsum('qhgd,nhd->hgqn', query_block.astype(jnp.float32), key_heads) * (1.0 / math.sqrt(HD))
    if mask is not None:
        scores = jnp.where(mask, scores, NEG)
    peak = lax.optimization_barrier(jnp.max(scores, axis=-1, keepdims=True))
    weights = jnp.exp(scores - peak)
    total = lax.optimization_barrier(jnp.sum(weights, axis=-1))
    rounded = lax.optimization_barrier(weights.astype(jnp.bfloat16)).astype(jnp.float32)
    mixed = jnp.einsum('hgqn,nhd->qhgd', rounded, value_heads)
    peak = jnp.transpose(peak[..., 0], (2, 0, 1))
    total = jnp.transpose(total, (2, 0, 1))
    peak = jnp.where(valid, peak, NEG)
    total = jnp.where(valid, total, 0.0)
    mixed = jnp.where(valid, mixed, 0.0)
    return (peak, total, mixed)

def combine(first, second):
    peak = jnp.maximum(first[0], second[0])
    left = jnp.exp(first[0] - peak)
    right = jnp.exp(second[0] - peak)
    return (peak, first[1] * left + second[1] * right, first[2] * left[..., None] + second[2] * right[..., None])

def reference(queries, own_cache, tree_cache, shared_cache, parent, leaf):
    group = QH // KVH

    def one_branch(items):
        query_rows, own_keys, own_values, leaf_id = items
        block_ids = path_of(leaf_id, parent)
        valid = block_ids >= 0
        depth = jnp.sum(valid.astype(jnp.int32)).astype(jnp.int32)
        offsets = jnp.arange(BQ, dtype=jnp.int32)
        positions = (BT * (depth + 1) + offsets).astype(jnp.int32)
        turned = rotate(query_rows.reshape(BQ, QH, HD).astype(jnp.float32), positions).astype(jnp.bfloat16)
        turned = turned.reshape(BQ, KVH, group, HD)
        own_turned = rotate(own_keys.reshape(BQ, KVH, HD).astype(jnp.float32), positions).astype(jnp.bfloat16)
        own_turned = own_turned.reshape(BQ, KVH * HD)
        state = block_terms(turned, shared_cache[0], shared_cache[1], True, None)
        for slot in range(SUB):
            start = (jnp.maximum(block_ids[slot], 0) * BT).astype(jnp.int32)
            keys = lax.dynamic_slice_in_dim(tree_cache[0], start, BT, 0)
            values = lax.dynamic_slice_in_dim(tree_cache[1], start, BT, 0)
            state = combine(state, block_terms(turned, keys, values, valid[slot], None))
        causal = offsets[:, None] >= offsets[None, :]
        state = combine(state, block_terms(turned, own_turned, own_values, True, causal))
        mixed = state[2] / state[1][..., None]
        return mixed.reshape(BQ, QH * HD).astype(jnp.bfloat16)
    items = (queries.reshape(BRANCHES, BQ, QH * HD), own_cache[0].reshape(BRANCHES, BQ, KVH * HD), own_cache[1].reshape(BRANCHES, BQ, KVH * HD), leaf)
    return lax.map(one_branch, items).reshape(QROWS, QH * HD)
```

```python
import math

import jax
import jax.numpy as jnp
import numpy as np
from jax import lax
from jax.experimental import pallas as pl
from jax.experimental.pallas import tpu as pltpu
from jax.sharding import PartitionSpec as P

HD = 128
BT = 512
BQ = 128
SUB = 8
BLK_DEV = 2
BR_DEV = 2
RING = 4
GROUP = 8
COLS = GROUP * BQ
TILE = 256
AHEAD = 2
LAG = 1
ONES = 16

BASE = 1000000.0
NEG = -1e30
MESH = pl.DeviceIdType.MESH

SHARED = 2
FAR = 3
FAR_EVEN = 10
SLOTS = 11
FIRST = 3
REMOTE = 7
BACK = {0: 0, 1: -1, 3: 7, 4: 2, 5: 1, 6: 6, 7: 5, 8: 4, 9: 3}
BEHIND = {4: 2, 5: 1, 6: 6, 7: 5, 8: 4, 9: 3, 3: 7, 0: 0, 1: -1}


def attention_kernel(
    nodes,
    parent,
    leaf,
    inverse,
    queries,
    own_cache,
    tree_cache,
    shared_cache,
    out,
    raw,
    turned,
    own,
    own_keys,
    kbuf,
    vbuf,
    peaks,
    totals,
    acc,
    obuf,
    live,
    load_sem,
    own_sem,
    local_k,
    local_v,
    z_send,
    up_send,
    down_send,
    relay_up_send,
    relay_down_send,
    recv_k,
    recv_v,
    out_send,
    out_recv,
    out_local,
):
    node = lax.axis_index("node")
    head = lax.axis_index("head")
    heads = 4
    y = lax.rem(node, RING)
    plane = node - y
    up = plane + lax.rem(y + 1, RING)
    down = plane + lax.rem(y + RING - 1, RING)
    after = lax.rem(node + 1, nodes)
    before = lax.rem(node + nodes - 1, nodes)
    ahead = lax.rem(node + RING, nodes)
    behind = lax.rem(node + nodes - RING, nodes)
    others = [lax.rem(head + k, heads) for k in range(1, heads)]

    def local_tree(g, blk):
        rows = pl.ds(blk * BT, BT)
        columns = pl.ds(g * HD, HD)
        return (
            pltpu.make_async_copy(tree_cache.at[0, rows, columns], kbuf.at[g, blk], local_k.at[g, blk]),
            pltpu.make_async_copy(tree_cache.at[1, rows, columns], vbuf.at[g, blk], local_v.at[g, blk]),
        )

    def local_shared(g):
        columns = pl.ds(g * HD, HD)
        return (
            pltpu.make_async_copy(shared_cache.at[0, :, columns], kbuf.at[g, SHARED], local_k.at[g, SHARED]),
            pltpu.make_async_copy(shared_cache.at[1, :, columns], vbuf.at[g, SHARED], local_v.at[g, SHARED]),
        )

    load_queries = pltpu.make_async_copy(queries, raw, load_sem)
    load_own = pltpu.make_async_copy(own_cache, own, own_sem)
    for g in range(2):
        for blk in range(2):
            for copy in local_tree(g, blk):
                copy.start()
    load_queries.start()
    load_own.start()
    for g in range(2):
        for copy in local_shared(g):
            copy.start()

    barrier = pltpu.get_barrier_semaphore()
    for source in (down, up, behind, before, after):
        pl.semaphore_signal(barrier, inc=1, device_id=(source, head), device_id_type=MESH)
    for other in others:
        pl.semaphore_signal(barrier, inc=1, device_id=(node, other), device_id_type=MESH)
    pl.semaphore_wait(barrier, 8)

    bufs = (kbuf, vbuf)
    recvs = (recv_k, recv_v)

    def remote(kv, g, source, target, sem, device):
        return pltpu.make_async_remote_copy(
            src_ref=bufs[kv].at[g, source],
            dst_ref=bufs[kv].at[g, target],
            send_sem=sem,
            recv_sem=recvs[kv].at[g, target],
            device_id=(device, head),
            device_id_type=MESH,
        )

    far_slot = (FAR_EVEN, FAR)
    passes_up = y == RING - 1
    passes_down = y > 0

    def z_copy(g, kv, blk):
        return remote(kv, g, blk, far_slot[blk], z_send.at[g, kv, blk], ahead)

    def up_copy(g, kv, blk):
        source = jnp.where(passes_up, far_slot[blk], blk)
        return remote(kv, g, source, 4 + blk, up_send.at[g, kv, blk], up)

    def down_copy(g, kv, blk):
        source = jnp.where(passes_down, far_slot[blk], blk)
        return remote(kv, g, source, 6 + blk, down_send.at[g, kv, blk], down)

    def relay_up(g, blk):
        return remote(0, g, 4 + blk, 8 + blk, relay_up_send.at[g, blk], after)

    def relay_down(g, blk):
        return remote(1, g, 6 + blk, 8 + blk, relay_down_send.at[g, blk], before)

    def arrived(g, kv, slot):
        pltpu.make_async_copy(bufs[kv].at[g, slot], bufs[kv].at[g, slot], recvs[kv].at[g, slot]).wait()

    chunks = ((0, 1), (1, 1), (0, 0), (1, 0))

    def send_own(g):
        for kv, blk in chunks:
            z_copy(g, kv, blk).start()

            @pl.when(jnp.logical_not(passes_up))
            def _():
                up_copy(g, kv, blk).start()

            @pl.when(jnp.logical_not(passes_down))
            def _():
                down_copy(g, kv, blk).start()

    def forward(g, chunk):
        kv, blk = chunks[chunk]
        arrived(g, kv, far_slot[blk])

        @pl.when(passes_down)
        def _():
            down_copy(g, kv, blk).start()

        @pl.when(passes_up)
        def _():
            up_copy(g, kv, blk).start()

    def pass_up(g, blk):
        arrived(g, 0, 4 + blk)
        relay_up(g, blk).start()

    def pass_down(g, blk):
        arrived(g, 1, 6 + blk)
        relay_down(g, blk).start()

    for g in range(2):
        for blk in range(2):
            for copy in local_tree(g, blk):
                copy.wait()
    send_own(0)

    ids = {slot: lax.rem(node * BLK_DEV + nodes * BLK_DEV - back, nodes * BLK_DEV) for slot, back in BACK.items()}
    depths = []
    for b in range(BR_DEV):
        current = leaf[b]
        depth = jnp.int32(0)
        hits = {slot: jnp.int32(0) for slot in ids}
        for step in range(SUB):
            valid = current >= 0
            depth = depth + valid.astype(jnp.int32)
            for slot, block in ids.items():
                hits[slot] = hits[slot] + (current == block).astype(jnp.int32)
            current = jnp.where(valid, parent[jnp.maximum(current, 0)], -1)
        depths.append(depth)
        for slot in ids:
            live[b, slot] = hits[slot]
        live[b, SHARED] = jnp.int32(1)

    load_queries.wait()
    load_own.wait()
    offsets = lax.broadcasted_iota(jnp.int32, (BQ, HD), 0)
    lane = lax.broadcasted_iota(jnp.int32, (BQ, HD), 1)
    factor = math.log2(math.e) / math.sqrt(HD)
    for b in range(BR_DEV):
        position = BT * (depths[b] + 1) + offsets
        angle = position.astype(jnp.float32) * inverse[...]
        cosine = jnp.cos(angle)
        sine = jnp.sin(angle)
        sine = jnp.where(lane < HD // 2, -sine, sine)

        def rotate(field):
            return field * cosine + pltpu.roll(field, HD // 2, 1) * sine

        rows = pl.ds(b * BQ, BQ)
        for g in range(2):
            for h in range(GROUP):
                field = raw[rows, (g * GROUP + h) * HD : (g * GROUP + h + 1) * HD].astype(jnp.float32)
                turned[g, b, h * BQ : (h + 1) * BQ, :] = (rotate(field) * factor).astype(jnp.bfloat16)
            field = own[0, rows, g * HD : (g + 1) * HD].astype(jnp.float32)
            own_keys[g, b] = rotate(field).astype(jnp.bfloat16)

    def scores_of(keys, g, b, r):
        return lax.dot_general(
            keys,
            turned[g, b, r : r + TILE, :],
            (((1,), (1,)), ((), ())),
            preferred_element_type=jnp.float32,
        )

    def with_ones(values):
        return jnp.concatenate([values.T, jnp.ones((ONES, values.shape[0]), jnp.bfloat16)], axis=0)

    def weigh(values, weights):
        return lax.dot_general(
            values, weights, (((1,), (0,)), ((), ())), preferred_element_type=jnp.float32
        )

    for g in range(2):
        for b in range(BR_DEV):
            keys = own_keys[g, b]
            values = with_ones(own[1, b * BQ : (b + 1) * BQ, g * HD : (g + 1) * HD])
            for r in range(0, COLS, TILE):
                scores = scores_of(keys, g, b, r)
                key_at = lax.broadcasted_iota(jnp.int32, (BQ, TILE), 0)
                token = lax.rem(lax.broadcasted_iota(jnp.int32, (BQ, TILE), 1), BQ)
                scores = jnp.where(key_at <= token, scores, NEG)
                peak = jnp.max(scores, axis=0, keepdims=True)
                weights = jnp.exp2(scores - peak).astype(jnp.bfloat16)
                mixed = weigh(values, weights)
                peaks[g, b, 0:1, r : r + TILE] = peak
                totals[g, b, 0:1, r : r + TILE] = mixed[HD : HD + 1]
                acc[g, b, :, r : r + TILE] = mixed[:HD]

    tiles = [(b, r) for b in range(BR_DEV) for r in range(0, COLS, TILE)]

    def attend(g, slot):
        keys = kbuf[g, slot]
        values = with_ones(vbuf[g, slot])
        on = [live[b, slot] > 0 for b in range(BR_DEV)]

        def soften(b, r, scores):
            before_peak = peaks[g, b, 0:1, r : r + TILE]
            peak = jnp.maximum(before_peak, jnp.where(on[b], jnp.max(scores, axis=0, keepdims=True), NEG))
            peaks[g, b, 0:1, r : r + TILE] = peak
            shift = jnp.where(on[b], peak, -NEG)
            weights = jnp.exp2(scores - shift).astype(jnp.bfloat16)
            return weights, jnp.exp2(before_peak - peak)

        def add(b, r, weights, fade):
            mixed = weigh(values, weights)
            acc[g, b, :, r : r + TILE] = acc[g, b, :, r : r + TILE] * fade + mixed[:HD]
            totals[g, b, 0:1, r : r + TILE] = totals[g, b, 0:1, r : r + TILE] * fade + mixed[HD : HD + 1]

        ready = [scores_of(keys, g, *tile) for tile in tiles[:AHEAD]]
        waiting = []
        for at, tile in enumerate(tiles):
            if at + AHEAD < len(tiles):
                ready.append(scores_of(keys, g, *tiles[at + AHEAD]))
            waiting.append(tile + soften(*tile, ready[at]))
            ready[at] = None
            if len(waiting) > LAG:
                add(*waiting.pop(0))
        for item in waiting:
            add(*item)

    def finish(g):
        for b in range(BR_DEV):
            for h in range(GROUP):
                span = slice(h * BQ, (h + 1) * BQ)
                mixed = acc[g, b, :, span] / totals[g, b, 0:1, span]
                obuf[b * BQ : (b + 1) * BQ, (g * GROUP + h) * HD : (g * GROUP + h + 1) * HD] = mixed.T.astype(
                    jnp.bfloat16
                )

    part = BR_DEV * BQ // heads

    def out_copy(g, k):
        device = others[k - 1]
        return pltpu.make_async_remote_copy(
            src_ref=obuf.at[pl.ds(pl.multiple_of(device * part, part), part), pl.ds(g * COLS, COLS)],
            dst_ref=out.at[:, pl.ds(pl.multiple_of((head * 2 + g) * COLS, COLS), COLS)],
            send_sem=out_send.at[g, k - 1],
            recv_sem=out_recv.at[g, k - 1],
            device_id=(node, device),
            device_id_type=MESH,
        )

    def out_keep(g):
        return pltpu.make_async_copy(
            obuf.at[pl.ds(pl.multiple_of(head * part, part), part), pl.ds(g * COLS, COLS)],
            out.at[:, pl.ds(pl.multiple_of((head * 2 + g) * COLS, COLS), COLS)],
            out_local.at[g],
        )

    def exchange(g):
        for k in (2, 1, 3):
            out_copy(g, k).start()
        out_keep(g).start()

    for g in range(2):
        for copy in local_shared(g):
            copy.wait()

    def local_step(i, carry):
        attend(i // 3, lax.rem(i, 3))

        @pl.when(i == 0)
        def _():
            forward(0, 0)

        @pl.when(i == 1)
        def _():
            forward(0, 1)
            pass_up(0, 1)

        @pl.when(i == 2)
        def _():
            pass_down(0, 1)

        @pl.when(i == 3)
        def _():
            forward(0, 2)
            send_own(1)

        @pl.when(i == 4)
        def _():
            forward(0, 3)
            pass_up(0, 0)

        @pl.when(i == 5)
        def _():
            pass_down(0, 0)

        return carry

    lax.fori_loop(0, 6, local_step, 0)

    def first_step(i, carry):
        slot = FIRST + i

        @pl.when((i == 1) | (i == 2))
        def _():
            arrived(0, 1, slot)

        @pl.when((i == 3) | (i == 4))
        def _():
            arrived(0, 0, slot)

        @pl.when(i >= 5)
        def _():
            arrived(0, 0, slot)
            arrived(0, 1, slot)

        @pl.when(i == 2)
        def _():
            forward(1, 0)

        @pl.when(i == 3)
        def _():
            forward(1, 1)
            pass_up(1, 1)

        @pl.when(i == 4)
        def _():
            pass_down(1, 1)

        @pl.when(i == 5)
        def _():
            forward(1, 2)

        @pl.when(i == 6)
        def _():
            forward(1, 3)

        attend(0, slot)
        return carry

    lax.fori_loop(0, REMOTE, first_step, 0)
    pass_up(1, 0)
    pass_down(1, 0)
    finish(0)
    exchange(0)

    def second_step(i, carry):
        slot = FIRST + i

        @pl.when((i == 1) | (i == 2))
        def _():
            arrived(1, 1, slot)

        @pl.when((i == 3) | (i == 4))
        def _():
            arrived(1, 0, slot)

        @pl.when(i >= 5)
        def _():
            arrived(1, 0, slot)
            arrived(1, 1, slot)

        attend(1, slot)
        return carry

    lax.fori_loop(0, REMOTE, second_step, 0)
    finish(1)
    exchange(1)

    for g in range(2):
        for kv, blk in chunks:
            z_copy(g, kv, blk).wait_send()
            up_copy(g, kv, blk).wait_send()
            down_copy(g, kv, blk).wait_send()
        for blk in range(2):
            relay_up(g, blk).wait_send()
            relay_down(g, blk).wait_send()
        for k in range(1, heads):
            out_copy(g, k).wait()
        out_keep(g).wait()


def inverse_frequencies():
    half = HD // 2
    inverse = np.power(np.float64(BASE), -np.arange(half) * (2.0 / HD)).astype(np.float32)
    return np.concatenate([inverse, inverse])[None, :]


def per_device(queries, own_cache, tree_cache, shared_cache, parent, leaf):
    nodes = lax.axis_size("node")
    heads = lax.axis_size("head")
    rows = queries.shape[0]
    dma = pltpu.SemaphoreType.DMA
    anywhere = pl.BlockSpec(memory_space=pl.ANY)
    scalars = pl.BlockSpec(memory_space=pltpu.SMEM)

    def kernel(*refs):
        attention_kernel(nodes, *refs)

    return pl.pallas_call(
        kernel,
        out_shape=jax.ShapeDtypeStruct((rows // heads, queries.shape[1] * heads), jnp.bfloat16),
        in_specs=[
            scalars,
            scalars,
            pl.BlockSpec(memory_space=pltpu.VMEM),
            anywhere,
            anywhere,
            anywhere,
            anywhere,
        ],
        out_specs=anywhere,
        scratch_shapes=[
            pltpu.VMEM(queries.shape, jnp.bfloat16),
            pltpu.VMEM((2, BR_DEV, COLS, HD), jnp.bfloat16),
            pltpu.VMEM(own_cache.shape, jnp.bfloat16),
            pltpu.VMEM((2, BR_DEV, BQ, HD), jnp.bfloat16),
            pltpu.VMEM((2, SLOTS, BT, HD), jnp.bfloat16),
            pltpu.VMEM((2, SLOTS, BT, HD), jnp.bfloat16),
            pltpu.VMEM((2, BR_DEV, 8, COLS), jnp.float32),
            pltpu.VMEM((2, BR_DEV, 8, COLS), jnp.float32),
            pltpu.VMEM((2, BR_DEV, HD, COLS), jnp.float32),
            pltpu.VMEM(queries.shape, jnp.bfloat16),
            pltpu.SMEM((BR_DEV, 16), jnp.int32),
            dma,
            dma,
            dma((2, 3)),
            dma((2, 3)),
            dma((2, 2, 2)),
            dma((2, 2, 2)),
            dma((2, 2, 2)),
            dma((2, 2)),
            dma((2, 2)),
            dma((2, SLOTS)),
            dma((2, SLOTS)),
            dma((2, 3)),
            dma((2, 3)),
            dma((2,)),
        ],
        compiler_params=pltpu.CompilerParams(
            collective_id=0, has_side_effects=True, vmem_limit_bytes=48 * 1024 * 1024
        ),
        name="branch_attention",
    )(parent, leaf, jnp.asarray(inverse_frequencies()), queries, own_cache, tree_cache, shared_cache)


def solution(mesh):
    in_specs = (
        P("node", "head"),
        P(None, "node", "head"),
        P(None, "node", "head"),
        P(None, None, "head"),
        P(),
        P("node"),
    )
    out_specs = P(("node", "head"), None)
    return jax.shard_map(
        per_device, mesh=mesh, in_specs=in_specs, out_specs=out_specs, check_vma=False
    )
```

```python
import math

import jax
import jax.numpy as jnp
import numpy as np
from jax import lax
from jax.experimental import pallas as pl
from jax.experimental.pallas import tpu as pltpu
from jax.sharding import PartitionSpec as P

HD = 128
BT = 512
BQ = 128
SUB = 8
BLK_DEV = 2
BR_DEV = 2
RING = 4
GROUP = 8
COLS = GROUP * BQ
TILE = 256
AHEAD = 2
LAG = 1
ONES = 16

BASE = 1000000.0
NEG = -1e30
MESH = pl.DeviceIdType.MESH

SHARED = 2
FAR = (10, 3)
NEXT = (5, 4)
THIRD = (9, 6)
SECOND = (8, 7)
SLOTS = 11
FIRST = 3
REMOTE = 7
BACK = {0: 0, 1: -1, 3: 7, 4: 1, 5: 2, 6: 5, 9: 6, 7: 3, 8: 4}


def attention_kernel(
    nodes,
    parent_in,
    leaf_in,
    inverse_in,
    queries,
    own_cache,
    tree_cache,
    shared_cache,
    out,
    raw,
    turned,
    own,
    own_keys,
    kbuf,
    vbuf,
    peaks,
    totals,
    acc,
    obuf,
    parent,
    leaf,
    inverse,
    live,
    small_sem,
    load_sem,
    own_sem,
    local_k,
    local_v,
    z_send,
    up_send,
    down_send,
    relay_up_send,
    relay_down_send,
    recv_k,
    recv_v,
    out_send,
    out_recv,
    out_local,
):
    node = lax.axis_index("node")
    head = lax.axis_index("head")
    heads = 4
    y = lax.rem(node, RING)
    plane = node - y
    up = plane + lax.rem(y + 1, RING)
    down = plane + lax.rem(y + RING - 1, RING)
    after = lax.rem(node + 1, nodes)
    before = lax.rem(node + nodes - 1, nodes)
    ahead = lax.rem(node + RING, nodes)
    behind = lax.rem(node + nodes - RING, nodes)
    others = [lax.rem(head + k, heads) for k in range(1, heads)]

    def local_tree(g, blk):
        rows = pl.ds(blk * BT, BT)
        columns = pl.ds(g * HD, HD)
        return (
            pltpu.make_async_copy(tree_cache.at[0, rows, columns], kbuf.at[g, blk], local_k.at[g, blk]),
            pltpu.make_async_copy(tree_cache.at[1, rows, columns], vbuf.at[g, blk], local_v.at[g, blk]),
        )

    def local_shared(g):
        columns = pl.ds(g * HD, HD)
        return (
            pltpu.make_async_copy(shared_cache.at[0, :, columns], kbuf.at[g, SHARED], local_k.at[g, SHARED]),
            pltpu.make_async_copy(shared_cache.at[1, :, columns], vbuf.at[g, SHARED], local_v.at[g, SHARED]),
        )

    load_queries = pltpu.make_async_copy(queries, raw, load_sem)
    load_own = pltpu.make_async_copy(own_cache, own, own_sem)
    for g in range(2):
        for blk in range(2):
            for copy in local_tree(g, blk):
                copy.start()
    small = [
        pltpu.make_async_copy(parent_in, parent, small_sem.at[0]),
        pltpu.make_async_copy(leaf_in, leaf, small_sem.at[1]),
        pltpu.make_async_copy(inverse_in, inverse, small_sem.at[2]),
    ]
    for copy in small:
        copy.start()
    load_queries.start()
    load_own.start()
    for g in range(2):
        for copy in local_shared(g):
            copy.start()

    barrier = pltpu.get_barrier_semaphore()
    for source in (down, up, behind, before, after):
        pl.semaphore_signal(barrier, inc=1, device_id=(source, head), device_id_type=MESH)
    for other in others:
        pl.semaphore_signal(barrier, inc=1, device_id=(node, other), device_id_type=MESH)
    pl.semaphore_wait(barrier, 8)

    bufs = (kbuf, vbuf)
    recvs = (recv_k, recv_v)

    def remote(kv, g, source, target, sem, device):
        return pltpu.make_async_remote_copy(
            src_ref=bufs[kv].at[g, source],
            dst_ref=bufs[kv].at[g, target],
            send_sem=sem,
            recv_sem=recvs[kv].at[g, target],
            device_id=(device, head),
            device_id_type=MESH,
        )

    passes_up = y == RING - 1
    passes_down = y > 0

    def z_copy(g, kv, blk):
        return pltpu.make_async_remote_copy(
            src_ref=tree_cache.at[kv, pl.ds(blk * BT, BT), pl.ds(g * HD, HD)],
            dst_ref=bufs[kv].at[g, FAR[blk]],
            send_sem=z_send.at[g, kv, blk],
            recv_sem=recvs[kv].at[g, FAR[blk]],
            device_id=(ahead, head),
            device_id_type=MESH,
        )

    def up_copy(g, kv, blk):
        source = jnp.where(passes_up, FAR[blk], blk)
        return remote(kv, g, source, NEXT[blk], up_send.at[g, kv, blk], up)

    def down_copy(g, kv, blk):
        source = jnp.where(passes_down, FAR[blk], blk)
        return remote(kv, g, source, THIRD[blk], down_send.at[g, kv, blk], down)

    def relay_up(g, blk):
        return remote(0, g, NEXT[blk], SECOND[blk], relay_up_send.at[g, blk], after)

    def relay_down(g, blk):
        return remote(1, g, THIRD[blk], SECOND[blk], relay_down_send.at[g, blk], before)

    def arrived(g, kv, slot):
        pltpu.make_async_copy(bufs[kv].at[g, slot], bufs[kv].at[g, slot], recvs[kv].at[g, slot]).wait()

    values_first = ((1, 1), (1, 0), (0, 1), (0, 0))
    keys_first = ((0, 1), (0, 0), (1, 1), (1, 0))

    def send_far(g):
        for kv, blk in values_first:
            z_copy(g, kv, blk).start()

    def send_own(g):
        @pl.when(jnp.logical_not(passes_up))
        def _():
            for kv, blk in keys_first:
                up_copy(g, kv, blk).start()

        @pl.when(jnp.logical_not(passes_down))
        def _():
            for kv, blk in values_first:
                down_copy(g, kv, blk).start()

    def forward(g, chunk):
        kv, blk = values_first[chunk]
        arrived(g, kv, FAR[blk])

        @pl.when(passes_down)
        def _():
            down_copy(g, kv, blk).start()

        @pl.when(passes_up)
        def _():
            up_copy(g, kv, blk).start()

    def pass_up(g, blk, late):
        @pl.when((y == 0) if late else (y > 0))
        def _():
            arrived(g, 0, NEXT[blk])
            relay_up(g, blk).start()

    def pass_down(g, blk):
        arrived(g, 1, THIRD[blk])
        relay_down(g, blk).start()

    send_far(0)
    send_far(1)
    for g in range(2):
        for blk in range(2):
            for copy in local_tree(g, blk):
                copy.wait()
    send_own(0)

    for copy in small:
        copy.wait()

    order = [1 - head // 2, head // 2]

    ids = {slot: lax.rem(node * BLK_DEV + nodes * BLK_DEV - back, nodes * BLK_DEV) for slot, back in BACK.items()}
    depths = []
    for b in range(BR_DEV):
        current = leaf[order[b]]
        depth = jnp.int32(0)
        hits = {slot: jnp.int32(0) for slot in ids}
        for step in range(SUB):
            valid = current >= 0
            depth = depth + valid.astype(jnp.int32)
            for slot, block in ids.items():
                hits[slot] = hits[slot] + (current == block).astype(jnp.int32)
            current = jnp.where(valid, parent[jnp.maximum(current, 0)], -1)
        depths.append(depth)
        for slot in ids:
            live[b, slot] = hits[slot]
        live[b, SHARED] = jnp.int32(1)

    load_queries.wait()
    load_own.wait()
    offsets = lax.broadcasted_iota(jnp.int32, (BQ, HD), 0)
    lane = lax.broadcasted_iota(jnp.int32, (BQ, HD), 1)
    factor = math.log2(math.e) / math.sqrt(HD)
    for b in range(BR_DEV):
        position = BT * (depths[b] + 1) + offsets
        angle = position.astype(jnp.float32) * inverse[...]
        cosine = jnp.cos(angle)
        sine = jnp.sin(angle)
        sine = jnp.where(lane < HD // 2, -sine, sine)

        def rotate(field):
            return field * cosine + pltpu.roll(field, HD // 2, 1) * sine

        rows = pl.ds(pl.multiple_of(order[b] * BQ, BQ), BQ)
        for g in range(2):
            for h in range(GROUP):
                field = raw[rows, (g * GROUP + h) * HD : (g * GROUP + h + 1) * HD].astype(jnp.float32)
                turned[g, b, h * BQ : (h + 1) * BQ, :] = (rotate(field) * factor).astype(jnp.bfloat16)
            field = own[0, rows, g * HD : (g + 1) * HD].astype(jnp.float32)
            own_keys[g, b] = rotate(field).astype(jnp.bfloat16)

    def scores_of(keys, g, b, r):
        return lax.dot_general(
            keys,
            turned[g, b, r : r + TILE, :],
            (((1,), (1,)), ((), ())),
            preferred_element_type=jnp.float32,
        )

    def with_ones(values):
        return jnp.concatenate([values.T, jnp.ones((ONES, values.shape[0]), jnp.bfloat16)], axis=0)

    def weigh(values, weights):
        return lax.dot_general(
            values, weights, (((1,), (0,)), ((), ())), preferred_element_type=jnp.float32
        )

    for g in range(2):
        for b in range(BR_DEV):
            keys = own_keys[g, b]
            values = with_ones(own[1, pl.ds(pl.multiple_of(order[b] * BQ, BQ), BQ), g * HD : (g + 1) * HD])
            for r in range(0, COLS, TILE):
                scores = scores_of(keys, g, b, r)
                key_at = lax.broadcasted_iota(jnp.int32, (BQ, TILE), 0)
                token = lax.rem(lax.broadcasted_iota(jnp.int32, (BQ, TILE), 1), BQ)
                scores = jnp.where(key_at <= token, scores, NEG)
                peak = jnp.max(scores, axis=0, keepdims=True)
                weights = jnp.exp2(scores - peak).astype(jnp.bfloat16)
                mixed = weigh(values, weights)
                peaks[g, b, 0:1, r : r + TILE] = peak
                totals[g, b, 0:1, r : r + TILE] = mixed[HD : HD + 1]
                acc[g, b, :, r : r + TILE] = mixed[:HD]

    def attend(g, slot, branches=range(BR_DEV)):
        tiles = [(b, r) for b in branches for r in range(0, COLS, TILE)]
        keys = kbuf[g, slot]
        values = with_ones(vbuf[g, slot])
        on = [live[b, slot] > 0 for b in range(BR_DEV)]

        def soften(b, r, scores):
            before_peak = peaks[g, b, 0:1, r : r + TILE]
            peak = jnp.maximum(before_peak, jnp.where(on[b], jnp.max(scores, axis=0, keepdims=True), NEG))
            peaks[g, b, 0:1, r : r + TILE] = peak
            shift = jnp.where(on[b], peak, -NEG)
            weights = jnp.exp2(scores - shift).astype(jnp.bfloat16)
            return weights, jnp.exp2(before_peak - peak)

        def add(b, r, weights, fade):
            mixed = weigh(values, weights)
            acc[g, b, :, r : r + TILE] = acc[g, b, :, r : r + TILE] * fade + mixed[:HD]
            totals[g, b, 0:1, r : r + TILE] = totals[g, b, 0:1, r : r + TILE] * fade + mixed[HD : HD + 1]

        ready = [scores_of(keys, g, *tile) for tile in tiles[:AHEAD]]
        waiting = []
        for at, tile in enumerate(tiles):
            if at + AHEAD < len(tiles):
                ready.append(scores_of(keys, g, *tiles[at + AHEAD]))
            waiting.append(tile + soften(*tile, ready[at]))
            ready[at] = None
            if len(waiting) > LAG:
                add(*waiting.pop(0))
        for item in waiting:
            add(*item)

    def finish(g, b):
        for h in range(GROUP):
            span = slice(h * BQ, (h + 1) * BQ)
            mixed = acc[g, b, :, span] / totals[g, b, 0:1, span]
            obuf[b * BQ : (b + 1) * BQ, (g * GROUP + h) * HD : (g * GROUP + h + 1) * HD] = mixed.T.astype(
                jnp.bfloat16
            )

    part = BR_DEV * BQ // heads

    def out_copy(g, b, j):
        device = order[b] * 2 + j
        at = lax.rem(device - head + heads, heads) - 1
        return pltpu.make_async_remote_copy(
            src_ref=obuf.at[pl.ds(b * BQ + j * part, part), pl.ds(g * COLS, COLS)],
            dst_ref=out.at[:, pl.ds(pl.multiple_of((head * 2 + g) * COLS, COLS), COLS)],
            send_sem=out_send.at[g, at],
            recv_sem=out_recv.at[g, at],
            device_id=(node, device),
            device_id_type=MESH,
        )

    core = lax.rem(head, 2)

    def out_keep(g):
        return pltpu.make_async_copy(
            obuf.at[pl.ds(pl.multiple_of(BQ + core * part, part), part), pl.ds(g * COLS, COLS)],
            out.at[:, pl.ds(pl.multiple_of((head * 2 + g) * COLS, COLS), COLS)],
            out_local.at[g],
        )

    def exchange(g, b):
        if b == 0:
            for j in range(2):
                out_copy(g, 0, j).start()
        else:
            out_copy(g, 1, 1 - core).start()
            out_keep(g).start()

    for g in range(2):
        for copy in local_shared(g):
            copy.wait()

    def at(i, step, *services):
        @pl.when(i == step)
        def _():
            for service in services:
                service()

    def first_step(i, carry):
        local = i < 6
        g = jnp.where(local, i // 3, 0)
        slot = jnp.where(local, lax.rem(i, 3), i - 6 + FIRST)
        at(i, 1, lambda: forward(0, 0), lambda: pass_up(0, 1, False))
        at(i, 3, lambda: forward(0, 1), lambda: pass_up(0, 0, False))
        at(i, 4, lambda: pass_down(0, 1))
        at(i, 5, lambda: forward(0, 2))
        at(i, 6, lambda: pass_down(0, 0))
        at(i, 7, lambda: forward(0, 3), lambda: pass_up(0, 1, True), lambda: arrived(0, 1, NEXT[1]))
        at(i, 8, lambda: forward(1, 0), lambda: pass_up(0, 0, True), lambda: arrived(0, 1, NEXT[0]))
        at(i, 9, lambda: send_own(1), lambda: arrived(0, 0, THIRD[1]))
        at(i, 10, lambda: forward(1, 1), lambda: arrived(0, 0, SECOND[1]), lambda: arrived(0, 1, SECOND[1]))
        at(i, 11, lambda: arrived(0, 0, SECOND[0]), lambda: arrived(0, 1, SECOND[0]))
        at(i, 12, lambda: forward(1, 2), lambda: arrived(0, 0, THIRD[0]))
        attend(g, slot)
        return carry

    lax.fori_loop(0, 6 + REMOTE, first_step, 0)
    forward(1, 3)
    pass_up(1, 1, False)
    for b in range(BR_DEV):
        finish(0, b)
        exchange(0, b)

    def second_step(i, carry):
        slot = jnp.where(i < 4, FIRST + i, jnp.where(i == 4, THIRD[0], FIRST + i - 1))
        at(i, 0, lambda: pass_up(1, 0, False), lambda: pass_down(1, 1))
        at(i, 1, lambda: pass_down(1, 0), lambda: pass_up(1, 1, True), lambda: arrived(1, 1, NEXT[1]))
        at(i, 2, lambda: pass_up(1, 0, True), lambda: arrived(1, 1, NEXT[0]))
        at(i, 3, lambda: arrived(1, 0, THIRD[1]))
        at(i, 4, lambda: arrived(1, 0, THIRD[0]))
        at(i, 5, lambda: arrived(1, 0, SECOND[1]), lambda: arrived(1, 1, SECOND[1]))
        attend(1, slot)
        return carry

    lax.fori_loop(0, REMOTE - 1, second_step, 0)
    arrived(1, 0, SECOND[0])
    arrived(1, 1, SECOND[0])
    for b in range(BR_DEV):
        attend(1, SECOND[0], (b,))
        finish(1, b)
        exchange(1, b)

    for g in range(2):
        for kv, blk in values_first:
            z_copy(g, kv, blk).wait_send()
            up_copy(g, kv, blk).wait_send()
            down_copy(g, kv, blk).wait_send()
        for blk in range(2):
            relay_up(g, blk).wait_send()
            relay_down(g, blk).wait_send()
        for j in range(2):
            out_copy(g, 0, j).wait()
        out_copy(g, 1, 1 - core).wait()
        out_keep(g).wait()


def inverse_frequencies():
    half = HD // 2
    inverse = np.power(np.float64(BASE), -np.arange(half) * (2.0 / HD)).astype(np.float32)
    return np.concatenate([inverse, inverse])[None, :]


def per_device(queries, own_cache, tree_cache, shared_cache, parent, leaf):
    nodes = lax.axis_size("node")
    heads = lax.axis_size("head")
    rows = queries.shape[0]
    dma = pltpu.SemaphoreType.DMA
    anywhere = pl.BlockSpec(memory_space=pl.ANY)

    def kernel(*refs):
        attention_kernel(nodes, *refs)

    return pl.pallas_call(
        kernel,
        out_shape=jax.ShapeDtypeStruct((rows // heads, queries.shape[1] * heads), jnp.bfloat16),
        in_specs=[anywhere] * 7,
        out_specs=anywhere,
        scratch_shapes=[
            pltpu.VMEM(queries.shape, jnp.bfloat16),
            pltpu.VMEM((2, BR_DEV, COLS, HD), jnp.bfloat16),
            pltpu.VMEM(own_cache.shape, jnp.bfloat16),
            pltpu.VMEM((2, BR_DEV, BQ, HD), jnp.bfloat16),
            pltpu.VMEM((2, SLOTS, BT, HD), jnp.bfloat16),
            pltpu.VMEM((2, SLOTS, BT, HD), jnp.bfloat16),
            pltpu.VMEM((2, BR_DEV, 8, COLS), jnp.float32),
            pltpu.VMEM((2, BR_DEV, 8, COLS), jnp.float32),
            pltpu.VMEM((2, BR_DEV, HD, COLS), jnp.float32),
            pltpu.VMEM(queries.shape, jnp.bfloat16),
            pltpu.SMEM(parent.shape, jnp.int32),
            pltpu.SMEM(leaf.shape, jnp.int32),
            pltpu.VMEM((1, HD), jnp.float32),
            pltpu.SMEM((BR_DEV, 16), jnp.int32),
            dma((3,)),
            dma,
            dma,
            dma((2, 3)),
            dma((2, 3)),
            dma((2, 2, 2)),
            dma((2, 2, 2)),
            dma((2, 2, 2)),
            dma((2, 2)),
            dma((2, 2)),
            dma((2, SLOTS)),
            dma((2, SLOTS)),
            dma((2, 3)),
            dma((2, 3)),
            dma((2,)),
        ],
        compiler_params=pltpu.CompilerParams(
            collective_id=0, has_side_effects=True, vmem_limit_bytes=64 * 1024 * 1024 - 64 * 1024
        ),
        name="branch_attention",
    )(parent, leaf, jnp.asarray(inverse_frequencies()), queries, own_cache, tree_cache, shared_cache)


def solution(mesh):
    in_specs = (
        P("node", "head"),
        P(None, "node", "head"),
        P(None, "node", "head"),
        P(None, None, "head"),
        P(),
        P("node"),
    )
    out_specs = P(("node", "head"), None)
    return jax.shard_map(
        per_device, mesh=mesh, in_specs=in_specs, out_specs=out_specs, check_vma=False
    )
```

```python
import math

import jax
import jax.numpy as jnp
import numpy as np
from jax import lax
from jax.experimental import pallas as pl
from jax.experimental.pallas import tpu as pltpu
from jax.sharding import PartitionSpec as P

HD = 128
BT = 512
BQ = 128
SUB = 8
BLK_DEV = 2
BR_DEV = 2
RING = 4
GROUP = 8
COLS = GROUP * BQ
TILE = 256
AHEAD = 2
LAG = 1
ONES = 16
PIECES = 1

BASE = 1000000.0
NEG = -1e30
MESH = pl.DeviceIdType.MESH

SHARED = 2
FAR = (10, 3)
NEXT = (5, 4)
THIRD = (9, 6)
SECOND = (8, 7)
SLOTS = 11
FIRST = 3
REMOTE = 7
BACK = {0: 0, 1: -1, 3: 7, 4: 1, 5: 2, 6: 5, 9: 6, 7: 3, 8: 4}

PLAN = {
    0: (
        (0, (("far", 1, 1, 1),)),
        (1, (("up", 0, 1, 0), ("down", 0, 1, 1), ("up", 1, 1, 0), ("far", 0, 0, 1),)),
        (3, (("up", 0, 0, 0),)),
        (4, (("down", 0, 0, 0), ("up", 0, 1, 1),)),
        (5, (("up", 0, 0, 1), ("down", 0, 0, 1),)),
        (6, (("values", 0, 1), ("down", 0, 1, 0), ("up", 1, 1, 1),)),
        (7, (("up", 1, 0, 0),)),
        (8, (("far", 0, 1, 1), ("down", 1, 0, 1),)),
        (10, (("far", 1, 0, 1),)),
        (11, (("down", 1, 1, 0),)),
        (12, (("down", 1, 1, 1),)),
        (13, (("down", 1, 0, 0),)),
        (14, (("up", 1, 0, 1), ("keys", 0, 1),)),
        (15, (("values", 1, 1),)),
        (19, (("values", 0, 0),)),
        (20, (("keys", 1, 0), ("values", 1, 0), ("keys", 1, 1),)),
        (21, (("keys", 0, 0),)),
    ),
    1: (
        (0, (("far", 0, 1, 0), ("far", 0, 1, 1),)),
        (1, (("up", 0, 0, 0), ("far", 0, 0, 1), ("up", 0, 1, 0),)),
        (2, (("far", 0, 0, 0), ("on", 0, 1, 0), ("far", 1, 1, 0), ("far", 1, 1, 1),)),
        (3, (("up", 0, 0, 1), ("on", 0, 1, 1),)),
        (4, (("up", 0, 1, 1), ("keys", 0, 0),)),
        (5, (("far", 1, 0, 0), ("values", 0, 0), ("up", 1, 1, 1),)),
        (7, (("on", 0, 0, 1), ("on", 0, 0, 0),)),
        (8, (("far", 1, 0, 1),)),
        (11, (("on", 1, 1, 0), ("up", 1, 1, 0), ("up", 1, 0, 0),)),
        (12, (("up", 1, 0, 1), ("on", 1, 1, 1),)),
        (14, (("on", 1, 0, 0),)),
        (16, (("keys", 1, 1), ("values", 1, 1),)),
        (17, (("keys", 1, 0),)),
        (18, (("keys", 0, 1),)),
        (20, (("values", 1, 0),)),
        (21, (("on", 1, 0, 1), ("values", 0, 1),)),
    ),
    3: (
        (0, (("far", 0, 1, 0), ("far", 0, 1, 1),)),
        (2, (("far", 0, 0, 1), ("on", 0, 1, 0),)),
        (3, (("keys", 0, 0), ("far", 0, 0, 0), ("values", 0, 1),)),
        (4, (("on", 0, 1, 1),)),
        (6, (("far", 1, 1, 1),)),
        (7, (("on", 0, 0, 1), ("far", 1, 1, 0),)),
        (9, (("on", 0, 0, 0), ("far", 1, 0, 1),)),
        (10, (("far", 1, 0, 0),)),
        (11, (("on", 1, 1, 1),)),
        (12, (("values", 0, 0),)),
        (14, (("on", 1, 1, 0),)),
        (16, (("on", 1, 0, 0),)),
        (17, (("keys", 0, 1), ("values", 1, 1), ("keys", 1, 0),)),
        (18, (("values", 1, 0),)),
        (20, (("keys", 1, 1),)),
        (21, (("on", 1, 0, 1),)),
    ),
}
FIRST_ORDER = (4, 6, 9, 5, 3, 7, 8)
SECOND_ORDER = (3, 4, 9, 6, 5, 7, 8)


def planned_steps(place, blocks):
    waited, sent = set(), set()
    steps = [[] for _ in range(len(blocks) + 2)]

    def wait(actions, *key):
        if key not in waited:
            waited.add(key)
            actions.append(("wait",) + key)

    def send(actions, op, g, *rest):
        if (op, g) + rest in sent:
            return
        if op == "values" and not any(other[0] == "values" for other in sent):
            actions.append(("ready", g))
        sent.add((op, g) + rest)
        for piece in range(PIECES):
            if op == "on":
                kv, blk = rest
                wait(actions, g, kv, FAR[blk], piece)
                actions.append(("down", g, kv, blk, piece))
                if place == 3:
                    actions.append(("up", g, kv, blk, piece))
            else:
                if op == "keys":
                    wait(actions, g, 0, NEXT[rest[0]], piece)
                elif op == "values":
                    wait(actions, g, 1, THIRD[rest[0]], piece)
                actions.append((op, g) + rest + (piece,))

    early = {step: ops for step, ops in PLAN[place]}
    for step, actions in enumerate(steps):
        for op in early.get(step, ()):
            send(actions, *op)
        if step < 2:
            continue
        if step == len(steps) - 1:
            for ops in early.values():
                for op in ops:
                    send(actions, *op)
        g, slot = blocks[step - 2]
        for blk in range(2):
            if slot == FAR[blk] and place != 0:
                send(actions, "on", g, 0, blk)
                send(actions, "on", g, 1, blk)
            if slot == NEXT[blk]:
                send(actions, "keys", g, blk)
            if slot == THIRD[blk]:
                send(actions, "values", g, blk)
        if slot >= FIRST:
            for kv in range(2):
                for piece in range(PIECES):
                    wait(actions, g, kv, slot, piece)
    return steps


def attention_kernel(
    nodes,
    parent_in,
    leaf_in,
    inverse_in,
    queries,
    own_cache,
    tree_cache,
    shared_cache,
    out,
    raw,
    turned,
    own,
    own_keys,
    kbuf,
    vbuf,
    peaks,
    totals,
    acc,
    obuf,
    parent,
    leaf,
    inverse,
    live,
    small_sem,
    ready_sem,
    load_sem,
    own_sem,
    local_k,
    local_v,
    z_send,
    up_send,
    down_send,
    relay_up_send,
    relay_down_send,
    recv_k,
    recv_v,
    out_send,
    out_recv,
    out_local,
):
    node = lax.axis_index("node")
    head = lax.axis_index("head")
    heads = 4
    y = lax.rem(node, RING)
    plane = node - y
    up = plane + lax.rem(y + 1, RING)
    down = plane + lax.rem(y + RING - 1, RING)
    after = lax.rem(node + 1, nodes)
    before = lax.rem(node + nodes - 1, nodes)
    ahead = lax.rem(node + RING, nodes)
    behind = lax.rem(node + nodes - RING, nodes)
    others = [lax.rem(head + k, heads) for k in range(1, heads)]

    barrier = pltpu.get_barrier_semaphore()
    for source in (down, up, behind, before):
        pl.semaphore_signal(barrier, inc=1, device_id=(source, head), device_id_type=MESH)
    for other in others:
        pl.semaphore_signal(barrier, inc=1, device_id=(node, other), device_id_type=MESH)

    def local_tree(g, blk):
        rows = pl.ds(blk * BT, BT)
        columns = pl.ds(g * HD, HD)
        return (
            pltpu.make_async_copy(tree_cache.at[0, rows, columns], kbuf.at[g, blk], local_k.at[g, blk]),
            pltpu.make_async_copy(tree_cache.at[1, rows, columns], vbuf.at[g, blk], local_v.at[g, blk]),
        )

    def local_shared(g):
        columns = pl.ds(g * HD, HD)
        return (
            pltpu.make_async_copy(shared_cache.at[0, :, columns], kbuf.at[g, SHARED], local_k.at[g, SHARED]),
            pltpu.make_async_copy(shared_cache.at[1, :, columns], vbuf.at[g, SHARED], local_v.at[g, SHARED]),
        )

    load_queries = pltpu.make_async_copy(queries, raw, load_sem)
    load_own = pltpu.make_async_copy(own_cache, own, own_sem)
    for g in range(2):
        for blk in range(2):
            for copy in local_tree(g, blk):
                copy.start()
    small = [
        pltpu.make_async_copy(parent_in, parent, small_sem.at[0]),
        pltpu.make_async_copy(leaf_in, leaf, small_sem.at[1]),
        pltpu.make_async_copy(inverse_in, inverse, small_sem.at[2]),
    ]
    for copy in small:
        copy.start()
    load_queries.start()
    load_own.start()
    for g in range(2):
        for copy in local_shared(g):
            copy.start()

    pl.semaphore_wait(barrier, 7)
    pl.semaphore_signal(ready_sem, inc=1, device_id=(after, head), device_id_type=MESH)

    bufs = (kbuf, vbuf)
    recvs = (recv_k, recv_v)

    def rows_of(piece):
        return pl.ds(piece * (BT // PIECES), BT // PIECES)

    def remote(kv, g, source, target, piece, sem, device):
        return pltpu.make_async_remote_copy(
            src_ref=bufs[kv].at[g, source, rows_of(piece)],
            dst_ref=bufs[kv].at[g, target, rows_of(piece)],
            send_sem=sem,
            recv_sem=recvs[kv].at[g, target, piece],
            device_id=(device, head),
            device_id_type=MESH,
        )

    passes_up = y == RING - 1
    passes_down = y > 0

    def z_copy(g, kv, blk, piece):
        rows = pl.ds(blk * BT + piece * (BT // PIECES), BT // PIECES)
        return pltpu.make_async_remote_copy(
            src_ref=tree_cache.at[kv, rows, pl.ds(g * HD, HD)],
            dst_ref=bufs[kv].at[g, FAR[blk], rows_of(piece)],
            send_sem=z_send.at[g, kv, blk, piece],
            recv_sem=recvs[kv].at[g, FAR[blk], piece],
            device_id=(ahead, head),
            device_id_type=MESH,
        )

    def up_copy(g, kv, blk, piece):
        source = jnp.where(passes_up, FAR[blk], blk)
        return remote(kv, g, source, NEXT[blk], piece, up_send.at[g, kv, blk, piece], up)

    def down_copy(g, kv, blk, piece):
        source = jnp.where(passes_down, FAR[blk], blk)
        return remote(kv, g, source, THIRD[blk], piece, down_send.at[g, kv, blk, piece], down)

    def relay_up(g, blk, piece):
        return remote(0, g, NEXT[blk], SECOND[blk], piece, relay_up_send.at[g, blk, piece], after)

    def relay_down(g, blk, piece):
        return remote(1, g, THIRD[blk], SECOND[blk], piece, relay_down_send.at[g, blk, piece], before)

    def arrived(g, kv, slot, piece):
        here = bufs[kv].at[g, slot, rows_of(piece)]
        pltpu.make_async_copy(here, here, recvs[kv].at[g, slot, piece]).wait()

    def act(op, g, *rest):
        if op == "wait":
            arrived(g, *rest)
        elif op == "far":
            z_copy(g, *rest).start()
        elif op == "up":
            up_copy(g, *rest).start()
        elif op == "down":
            down_copy(g, *rest).start()
        elif op == "keys":
            relay_up(g, *rest).start()
        elif op == "values":
            relay_down(g, *rest).start()
        else:
            pl.semaphore_wait(ready_sem, 1)

    blocks = [(g, slot) for g in range(2) for slot in range(3)]
    blocks += [(0, slot) for slot in FIRST_ORDER] + [(1, slot) for slot in SECOND_ORDER]
    plans = {place: planned_steps(place, blocks) for place in PLAN}
    at_place = {0: y == 0, 1: (y == 1) | (y == 2), 3: y == 3}

    def serve(step):
        for place, plan in plans.items():
            if plan[step]:

                @pl.when(at_place[place])
                def _():
                    for action in plan[step]:
                        act(*action)

    serve(0)
    for g in range(2):
        for blk in range(2):
            for copy in local_tree(g, blk):
                copy.wait()
    serve(1)

    for copy in small:
        copy.wait()

    order = [1 - head // 2, head // 2]

    ids = {slot: lax.rem(node * BLK_DEV + nodes * BLK_DEV - back, nodes * BLK_DEV) for slot, back in BACK.items()}
    depths = []
    for b in range(BR_DEV):
        current = leaf[order[b]]
        depth = jnp.int32(0)
        hits = {slot: jnp.int32(0) for slot in ids}
        for step in range(SUB):
            valid = current >= 0
            depth = depth + valid.astype(jnp.int32)
            for slot, block in ids.items():
                hits[slot] = hits[slot] + (current == block).astype(jnp.int32)
            current = jnp.where(valid, parent[jnp.maximum(current, 0)], -1)
        depths.append(depth)
        for slot in ids:
            live[b, slot] = hits[slot]
        live[b, SHARED] = jnp.int32(1)

    load_queries.wait()
    load_own.wait()
    offsets = lax.broadcasted_iota(jnp.int32, (BQ, HD), 0)
    lane = lax.broadcasted_iota(jnp.int32, (BQ, HD), 1)
    factor = math.log2(math.e) / math.sqrt(HD)
    for b in range(BR_DEV):
        position = BT * (depths[b] + 1) + offsets
        angle = position.astype(jnp.float32) * inverse[...]
        cosine = jnp.cos(angle)
        sine = jnp.sin(angle)
        sine = jnp.where(lane < HD // 2, -sine, sine)

        def rotate(field):
            return field * cosine + pltpu.roll(field, HD // 2, 1) * sine

        rows = pl.ds(pl.multiple_of(order[b] * BQ, BQ), BQ)
        for g in range(2):
            for h in range(GROUP):
                field = raw[rows, (g * GROUP + h) * HD : (g * GROUP + h + 1) * HD].astype(jnp.float32)
                turned[g, b, h * BQ : (h + 1) * BQ, :] = (rotate(field) * factor).astype(jnp.bfloat16)
            field = own[0, rows, g * HD : (g + 1) * HD].astype(jnp.float32)
            own_keys[g, b] = rotate(field).astype(jnp.bfloat16)

    def scores_of(keys, g, b, r):
        return lax.dot_general(
            keys,
            turned[g, b, r : r + TILE, :],
            (((1,), (1,)), ((), ())),
            preferred_element_type=jnp.float32,
        )

    def with_ones(values):
        return jnp.concatenate([values.T, jnp.ones((ONES, values.shape[0]), jnp.bfloat16)], axis=0)

    def weigh(values, weights):
        return lax.dot_general(
            values, weights, (((1,), (0,)), ((), ())), preferred_element_type=jnp.float32
        )

    for g in range(2):
        for b in range(BR_DEV):
            keys = own_keys[g, b]
            values = with_ones(own[1, pl.ds(pl.multiple_of(order[b] * BQ, BQ), BQ), g * HD : (g + 1) * HD])
            for r in range(0, COLS, TILE):
                scores = scores_of(keys, g, b, r)
                key_at = lax.broadcasted_iota(jnp.int32, (BQ, TILE), 0)
                token = lax.rem(lax.broadcasted_iota(jnp.int32, (BQ, TILE), 1), BQ)
                scores = jnp.where(key_at <= token, scores, NEG)
                peak = jnp.max(scores, axis=0, keepdims=True)
                weights = jnp.exp2(scores - peak).astype(jnp.bfloat16)
                mixed = weigh(values, weights)
                peaks[g, b, 0:1, r : r + TILE] = peak
                totals[g, b, 0:1, r : r + TILE] = mixed[HD : HD + 1]
                acc[g, b, :, r : r + TILE] = mixed[:HD]

    def attend(g, slot, branches=range(BR_DEV)):
        tiles = [(b, r) for b in branches for r in range(0, COLS, TILE)]
        keys = kbuf[g, slot]
        values = with_ones(vbuf[g, slot])
        on = [live[b, slot] > 0 for b in range(BR_DEV)]

        def soften(b, r, scores):
            before_peak = peaks[g, b, 0:1, r : r + TILE]
            peak = jnp.maximum(before_peak, jnp.where(on[b], jnp.max(scores, axis=0, keepdims=True), NEG))
            peaks[g, b, 0:1, r : r + TILE] = peak
            shift = jnp.where(on[b], peak, -NEG)
            weights = jnp.exp2(scores - shift).astype(jnp.bfloat16)
            return weights, jnp.exp2(before_peak - peak)

        def add(b, r, weights, fade):
            mixed = weigh(values, weights)
            acc[g, b, :, r : r + TILE] = acc[g, b, :, r : r + TILE] * fade + mixed[:HD]
            totals[g, b, 0:1, r : r + TILE] = totals[g, b, 0:1, r : r + TILE] * fade + mixed[HD : HD + 1]

        ready = [scores_of(keys, g, *tile) for tile in tiles[:AHEAD]]
        waiting = []
        for at, tile in enumerate(tiles):
            if at + AHEAD < len(tiles):
                ready.append(scores_of(keys, g, *tiles[at + AHEAD]))
            waiting.append(tile + soften(*tile, ready[at]))
            ready[at] = None
            if len(waiting) > LAG:
                add(*waiting.pop(0))
        for item in waiting:
            add(*item)

    def finish(g, b):
        for h in range(GROUP):
            span = slice(h * BQ, (h + 1) * BQ)
            mixed = acc[g, b, :, span] / totals[g, b, 0:1, span]
            obuf[b * BQ : (b + 1) * BQ, (g * GROUP + h) * HD : (g * GROUP + h + 1) * HD] = mixed.T.astype(
                jnp.bfloat16
            )

    part = BR_DEV * BQ // heads

    def out_copy(g, b, j):
        device = order[b] * 2 + j
        at = lax.rem(device - head + heads, heads) - 1
        return pltpu.make_async_remote_copy(
            src_ref=obuf.at[pl.ds(b * BQ + j * part, part), pl.ds(g * COLS, COLS)],
            dst_ref=out.at[:, pl.ds(pl.multiple_of((head * 2 + g) * COLS, COLS), COLS)],
            send_sem=out_send.at[g, at],
            recv_sem=out_recv.at[g, at],
            device_id=(node, device),
            device_id_type=MESH,
        )

    core = lax.rem(head, 2)

    def out_keep(g):
        return pltpu.make_async_copy(
            obuf.at[pl.ds(pl.multiple_of(BQ + core * part, part), part), pl.ds(g * COLS, COLS)],
            out.at[:, pl.ds(pl.multiple_of((head * 2 + g) * COLS, COLS), COLS)],
            out_local.at[g],
        )

    def exchange(g, b):
        if b == 0:
            for j in range(2):
                out_copy(g, 0, j).start()
        else:
            out_copy(g, 1, 1 - core).start()
            out_keep(g).start()

    for g in range(2):
        for copy in local_shared(g):
            copy.wait()

    def serve_at(i, steps):
        for step in steps:
            if any(plan[step + 2] for plan in plans.values()):

                @pl.when(i == step)
                def _():
                    serve(step + 2)

    def pick(i, values):
        result = jnp.int32(values[0])
        for at, value in enumerate(values[1:]):
            result = jnp.where(i == at + 1, value, result)
        return result

    first = 6 + REMOTE

    def first_step(i, carry):
        serve_at(i, range(first))
        attend(pick(i, [g for g, _ in blocks[:first]]), pick(i, [slot for _, slot in blocks[:first]]))
        return carry

    lax.fori_loop(0, first, first_step, 0)
    for b in range(BR_DEV):
        finish(0, b)
        exchange(0, b)

    last = len(blocks) - 1

    def second_step(i, carry):
        serve_at(i + first, range(first, last))
        attend(1, pick(i, SECOND_ORDER[:-1]))
        return carry

    lax.fori_loop(0, last - first, second_step, 0)
    serve(last + 2)
    for b in range(BR_DEV):
        attend(1, SECOND_ORDER[-1], (b,))
        finish(1, b)
        exchange(1, b)

    for g in range(2):
        for piece in range(PIECES):
            for blk in range(2):
                for kv in range(2):
                    up_copy(g, kv, blk, piece).wait_send()
                    down_copy(g, kv, blk, piece).wait_send()
                relay_up(g, blk, piece).wait_send()
                relay_down(g, blk, piece).wait_send()
            for kv in range(2):
                z_copy(g, kv, 1, piece).wait_send()

                @pl.when(y > 0)
                def _():
                    z_copy(g, kv, 0, piece).wait_send()

        for j in range(2):
            out_copy(g, 0, j).wait()
        out_copy(g, 1, 1 - core).wait()
        out_keep(g).wait()


def inverse_frequencies():
    half = HD // 2
    inverse = np.power(np.float64(BASE), -np.arange(half) * (2.0 / HD)).astype(np.float32)
    return np.concatenate([inverse, inverse])[None, :]


def per_device(queries, own_cache, tree_cache, shared_cache, parent, leaf):
    nodes = lax.axis_size("node")
    heads = lax.axis_size("head")
    rows = queries.shape[0]
    dma = pltpu.SemaphoreType.DMA
    anywhere = pl.BlockSpec(memory_space=pl.ANY)

    def kernel(*refs):
        attention_kernel(nodes, *refs)

    return pl.pallas_call(
        kernel,
        out_shape=jax.ShapeDtypeStruct((rows // heads, queries.shape[1] * heads), jnp.bfloat16),
        in_specs=[anywhere] * 7,
        out_specs=anywhere,
        scratch_shapes=[
            pltpu.VMEM(queries.shape, jnp.bfloat16),
            pltpu.VMEM((2, BR_DEV, COLS, HD), jnp.bfloat16),
            pltpu.VMEM(own_cache.shape, jnp.bfloat16),
            pltpu.VMEM((2, BR_DEV, BQ, HD), jnp.bfloat16),
            pltpu.VMEM((2, SLOTS, BT, HD), jnp.bfloat16),
            pltpu.VMEM((2, SLOTS, BT, HD), jnp.bfloat16),
            pltpu.VMEM((2, BR_DEV, 8, COLS), jnp.float32),
            pltpu.VMEM((2, BR_DEV, 8, COLS), jnp.float32),
            pltpu.VMEM((2, BR_DEV, HD, COLS), jnp.float32),
            pltpu.VMEM(queries.shape, jnp.bfloat16),
            pltpu.SMEM(parent.shape, jnp.int32),
            pltpu.SMEM(leaf.shape, jnp.int32),
            pltpu.VMEM((1, HD), jnp.float32),
            pltpu.SMEM((BR_DEV, 16), jnp.int32),
            dma((3,)),
            pltpu.SemaphoreType.REGULAR,
            dma,
            dma,
            dma((2, 3)),
            dma((2, 3)),
            dma((2, 2, 2, PIECES)),
            dma((2, 2, 2, PIECES)),
            dma((2, 2, 2, PIECES)),
            dma((2, 2, PIECES)),
            dma((2, 2, PIECES)),
            dma((2, SLOTS, PIECES)),
            dma((2, SLOTS, PIECES)),
            dma((2, 3)),
            dma((2, 3)),
            dma((2,)),
        ],
        compiler_params=pltpu.CompilerParams(
            collective_id=0, has_side_effects=True, vmem_limit_bytes=64 * 1024 * 1024 - 64 * 1024
        ),
        name="branch_attention",
    )(parent, leaf, jnp.asarray(inverse_frequencies()), queries, own_cache, tree_cache, shared_cache)


def solution(mesh):
    in_specs = (
        P("node", "head"),
        P(None, "node", "head"),
        P(None, "node", "head"),
        P(None, None, "head"),
        P(),
        P("node"),
    )
    out_specs = P(("node", "head"), None)
    return jax.shard_map(
        per_device, mesh=mesh, in_specs=in_specs, out_specs=out_specs, check_vma=False
    )
```

```python
import math

import jax
import jax.numpy as jnp
import numpy as np
from jax import lax
from jax.experimental import pallas as pl
from jax.experimental.pallas import tpu as pltpu
from jax.sharding import PartitionSpec as P

HD = 128
BT = 512
BQ = 128
SUB = 8
BLK_DEV = 2
BR_DEV = 2
RING = 4
GROUP = 8
COLS = GROUP * BQ
TILE = 256
AHEAD = 2
LAG = 1
ONES = 16
PIECES = 1

BASE = 1000000.0
NEG = -1e30
MESH = pl.DeviceIdType.MESH

SHARED = 2
FAR = (10, 3)
NEXT = (5, 4)
THIRD = (9, 6)
SECOND = (8, 7)
SLOTS = 11
FIRST = 3
REMOTE = 7
BACK = {0: 0, 1: -1, 3: 7, 4: 1, 5: 2, 6: 5, 9: 6, 7: 3, 8: 4}

PLAN = {
    0: (
        (0, (("far", 1, 1, 1),)),
        (1, (("up", 1, 1, 0), ("down", 0, 1, 1), ("down", 1, 0, 1), ("up", 0, 0, 1), ("up", 0, 1, 1),)),
        (2, (("far", 1, 0, 1),)),
        (3, (("down", 0, 0, 0), ("far", 0, 1, 1),)),
        (4, (("up", 1, 0, 1), ("up", 0, 1, 0), ("up", 1, 0, 0),)),
        (5, (("down", 0, 0, 1),)),
        (6, (("far", 0, 0, 1), ("down", 0, 1, 0), ("up", 0, 0, 0),)),
        (9, (("down", 1, 1, 0),)),
        (11, (("down", 1, 1, 1),)),
        (12, (("up", 1, 1, 1),)),
        (13, (("values", 1, 1), ("down", 1, 0, 0), ("keys", 0, 0),)),
        (14, (("values", 0, 1),)),
        (15, (("values", 1, 0),)),
        (17, (("keys", 1, 0), ("keys", 1, 1),)),
        (18, (("values", 0, 0),)),
        (19, (("keys", 0, 1),)),
    ),
    1: (
        (0, (("far", 0, 1, 1), ("far", 0, 0, 0),)),
        (1, (("up", 0, 0, 1), ("up", 1, 1, 0),)),
        (3, (("far", 0, 1, 0), ("on", 0, 1, 1), ("up", 0, 1, 1),)),
        (4, (("on", 0, 0, 0), ("up", 0, 0, 0), ("far", 0, 0, 1), ("far", 1, 1, 0),)),
        (5, (("up", 0, 1, 0), ("on", 0, 1, 0),)),
        (6, (("values", 0, 1),)),
        (7, (("far", 1, 1, 1), ("far", 1, 0, 0), ("up", 1, 0, 1),)),
        (9, (("far", 1, 0, 1),)),
        (11, (("keys", 0, 1),)),
        (12, (("on", 1, 1, 1), ("on", 1, 1, 0), ("keys", 1, 1),)),
        (14, (("up", 1, 0, 0), ("on", 1, 0, 0), ("up", 1, 1, 1), ("values", 0, 0), ("on", 0, 0, 1),)),
        (17, (("values", 1, 1),)),
        (18, (("keys", 1, 0),)),
        (19, (("values", 1, 0),)),
        (20, (("on", 1, 0, 1), ("keys", 0, 0),)),
    ),
    3: (
        (0, (("far", 0, 1, 1), ("far", 0, 0, 1),)),
        (2, (("values", 0, 1), ("far", 0, 1, 0),)),
        (3, (("on", 0, 1, 1),)),
        (4, (("far", 0, 0, 0),)),
        (5, (("on", 0, 0, 1), ("keys", 0, 1),)),
        (6, (("far", 1, 0, 0),)),
        (7, (("on", 0, 1, 0),)),
        (9, (("far", 1, 1, 0),)),
        (10, (("on", 0, 0, 0),)),
        (12, (("far", 1, 0, 1), ("on", 1, 0, 0), ("far", 1, 1, 1), ("on", 1, 1, 0),)),
        (14, (("on", 1, 0, 1), ("keys", 1, 1),)),
        (16, (("values", 1, 1),)),
        (18, (("values", 0, 0), ("on", 1, 1, 1),)),
        (20, (("keys", 1, 0),)),
        (21, (("keys", 0, 0), ("values", 1, 0),)),
    ),
}
FIRST_ORDER = (4, 3, 9, 5, 6, 8, 7)
SECOND_ORDER = (3, 5, 9, 6, 4, 7, 8)


def planned_steps(place, blocks):
    waited, sent = set(), set()
    steps = [[] for _ in range(len(blocks) + 2)]

    def wait(actions, *key):
        if key not in waited:
            waited.add(key)
            actions.append(("wait",) + key)

    def send(actions, op, g, *rest):
        if (op, g) + rest in sent:
            return
        if op == "values" and not any(other[0] == "values" for other in sent):
            actions.append(("ready", g))
        sent.add((op, g) + rest)
        for piece in range(PIECES):
            if op == "on":
                kv, blk = rest
                wait(actions, g, kv, FAR[blk], piece)
                actions.append(("down", g, kv, blk, piece))
                if place == 3:
                    actions.append(("up", g, kv, blk, piece))
            else:
                if op == "keys":
                    wait(actions, g, 0, NEXT[rest[0]], piece)
                elif op == "values":
                    wait(actions, g, 1, THIRD[rest[0]], piece)
                actions.append((op, g) + rest + (piece,))

    early = {step: ops for step, ops in PLAN[place]}
    for step, actions in enumerate(steps):
        for op in early.get(step, ()):
            send(actions, *op)
        if step < 2:
            continue
        if step == len(steps) - 1:
            for ops in early.values():
                for op in ops:
                    send(actions, *op)
        g, slot = blocks[step - 2]
        for blk in range(2):
            if slot == FAR[blk] and place != 0:
                send(actions, "on", g, 0, blk)
                send(actions, "on", g, 1, blk)
            if slot == NEXT[blk]:
                send(actions, "keys", g, blk)
            if slot == THIRD[blk]:
                send(actions, "values", g, blk)
        if slot >= FIRST:
            for kv in range(2):
                for piece in range(PIECES):
                    wait(actions, g, kv, slot, piece)
    return steps


def attention_kernel(
    nodes,
    parent_in,
    leaf_in,
    inverse_in,
    queries,
    own_cache,
    tree_cache,
    shared_cache,
    out,
    raw,
    turned,
    own,
    own_keys,
    kbuf,
    vbuf,
    peaks,
    totals,
    acc,
    obuf,
    parent,
    leaf,
    inverse,
    live,
    small_sem,
    ready_sem,
    load_sem,
    own_sem,
    local_k,
    local_v,
    z_send,
    up_send,
    down_send,
    relay_up_send,
    relay_down_send,
    recv_k,
    recv_v,
    out_send,
    out_recv,
    out_local,
):
    node = lax.axis_index("node")
    head = lax.axis_index("head")
    heads = 4
    y = lax.rem(node, RING)
    plane = node - y
    up = plane + lax.rem(y + 1, RING)
    down = plane + lax.rem(y + RING - 1, RING)
    after = lax.rem(node + 1, nodes)
    before = lax.rem(node + nodes - 1, nodes)
    ahead = lax.rem(node + RING, nodes)
    behind = lax.rem(node + nodes - RING, nodes)
    others = [lax.rem(head + k, heads) for k in range(1, heads)]

    barrier = pltpu.get_barrier_semaphore()
    for source in (down, up, behind, before):
        pl.semaphore_signal(barrier, inc=1, device_id=(source, head), device_id_type=MESH)
    for other in others:
        pl.semaphore_signal(barrier, inc=1, device_id=(node, other), device_id_type=MESH)

    def local_tree(g, blk):
        rows = pl.ds(blk * BT, BT)
        columns = pl.ds(g * HD, HD)
        return (
            pltpu.make_async_copy(tree_cache.at[0, rows, columns], kbuf.at[g, blk], local_k.at[g, blk]),
            pltpu.make_async_copy(tree_cache.at[1, rows, columns], vbuf.at[g, blk], local_v.at[g, blk]),
        )

    def local_shared(g):
        columns = pl.ds(g * HD, HD)
        return (
            pltpu.make_async_copy(shared_cache.at[0, :, columns], kbuf.at[g, SHARED], local_k.at[g, SHARED]),
            pltpu.make_async_copy(shared_cache.at[1, :, columns], vbuf.at[g, SHARED], local_v.at[g, SHARED]),
        )

    load_queries = pltpu.make_async_copy(queries, raw, load_sem)
    load_own = pltpu.make_async_copy(own_cache, own, own_sem)
    for g in range(2):
        for blk in range(2):
            for copy in local_tree(g, blk):
                copy.start()
    small = [
        pltpu.make_async_copy(parent_in, parent, small_sem.at[0]),
        pltpu.make_async_copy(leaf_in, leaf, small_sem.at[1]),
        pltpu.make_async_copy(inverse_in, inverse, small_sem.at[2]),
    ]
    for copy in small:
        copy.start()
    load_queries.start()
    load_own.start()
    for g in range(2):
        for copy in local_shared(g):
            copy.start()

    pl.semaphore_wait(barrier, 7)
    pl.semaphore_signal(ready_sem, inc=1, device_id=(after, head), device_id_type=MESH)

    bufs = (kbuf, vbuf)
    recvs = (recv_k, recv_v)

    def rows_of(piece):
        return pl.ds(piece * (BT // PIECES), BT // PIECES)

    def remote(kv, g, source, target, piece, sem, device):
        return pltpu.make_async_remote_copy(
            src_ref=bufs[kv].at[g, source, rows_of(piece)],
            dst_ref=bufs[kv].at[g, target, rows_of(piece)],
            send_sem=sem,
            recv_sem=recvs[kv].at[g, target, piece],
            device_id=(device, head),
            device_id_type=MESH,
        )

    passes_up = y == RING - 1
    passes_down = y > 0

    def z_copy(g, kv, blk, piece):
        rows = pl.ds(blk * BT + piece * (BT // PIECES), BT // PIECES)
        return pltpu.make_async_remote_copy(
            src_ref=tree_cache.at[kv, rows, pl.ds(g * HD, HD)],
            dst_ref=bufs[kv].at[g, FAR[blk], rows_of(piece)],
            send_sem=z_send.at[g, kv, blk, piece],
            recv_sem=recvs[kv].at[g, FAR[blk], piece],
            device_id=(ahead, head),
            device_id_type=MESH,
        )

    def up_copy(g, kv, blk, piece):
        source = jnp.where(passes_up, FAR[blk], blk)
        return remote(kv, g, source, NEXT[blk], piece, up_send.at[g, kv, blk, piece], up)

    def down_copy(g, kv, blk, piece):
        source = jnp.where(passes_down, FAR[blk], blk)
        return remote(kv, g, source, THIRD[blk], piece, down_send.at[g, kv, blk, piece], down)

    def relay_up(g, blk, piece):
        return remote(0, g, NEXT[blk], SECOND[blk], piece, relay_up_send.at[g, blk, piece], after)

    def relay_down(g, blk, piece):
        return remote(1, g, THIRD[blk], SECOND[blk], piece, relay_down_send.at[g, blk, piece], before)

    def arrived(g, kv, slot, piece):
        here = bufs[kv].at[g, slot, rows_of(piece)]
        pltpu.make_async_copy(here, here, recvs[kv].at[g, slot, piece]).wait()

    def act(op, g, *rest):
        if op == "wait":
            arrived(g, *rest)
        elif op == "far":
            z_copy(g, *rest).start()
        elif op == "up":
            up_copy(g, *rest).start()
        elif op == "down":
            down_copy(g, *rest).start()
        elif op == "keys":
            relay_up(g, *rest).start()
        elif op == "values":
            relay_down(g, *rest).start()
        else:
            pl.semaphore_wait(ready_sem, 1)

    blocks = [(g, slot) for g in range(2) for slot in range(3)]
    blocks += [(0, slot) for slot in FIRST_ORDER] + [(1, slot) for slot in SECOND_ORDER]
    plans = {place: planned_steps(place, blocks) for place in PLAN}
    at_place = {0: y == 0, 1: (y == 1) | (y == 2), 3: y == 3}

    def serve(step):
        for place, plan in plans.items():
            if plan[step]:

                @pl.when(at_place[place])
                def _():
                    for action in plan[step]:
                        act(*action)

    serve(0)
    for g in range(2):
        for blk in range(2):
            for copy in local_tree(g, blk):
                copy.wait()
    serve(1)

    for copy in small:
        copy.wait()

    order = [1 - head // 2, head // 2]

    ids = {slot: lax.rem(node * BLK_DEV + nodes * BLK_DEV - back, nodes * BLK_DEV) for slot, back in BACK.items()}
    depths = []
    for b in range(BR_DEV):
        current = leaf[order[b]]
        depth = jnp.int32(0)
        hits = {slot: jnp.int32(0) for slot in ids}
        for step in range(SUB):
            valid = current >= 0
            depth = depth + valid.astype(jnp.int32)
            for slot, block in ids.items():
                hits[slot] = hits[slot] + (current == block).astype(jnp.int32)
            current = jnp.where(valid, parent[jnp.maximum(current, 0)], -1)
        depths.append(depth)
        for slot in ids:
            live[b, slot] = hits[slot]
        live[b, SHARED] = jnp.int32(1)

    load_queries.wait()
    load_own.wait()
    offsets = lax.broadcasted_iota(jnp.int32, (BQ, HD), 0)
    lane = lax.broadcasted_iota(jnp.int32, (BQ, HD), 1)
    factor = math.log2(math.e) / math.sqrt(HD)
    for b in range(BR_DEV):
        position = BT * (depths[b] + 1) + offsets
        angle = position.astype(jnp.float32) * inverse[...]
        cosine = jnp.cos(angle)
        sine = jnp.sin(angle)
        sine = jnp.where(lane < HD // 2, -sine, sine)

        def rotate(field):
            return field * cosine + pltpu.roll(field, HD // 2, 1) * sine

        rows = pl.ds(pl.multiple_of(order[b] * BQ, BQ), BQ)
        for g in range(2):
            for h in range(GROUP):
                field = raw[rows, (g * GROUP + h) * HD : (g * GROUP + h + 1) * HD].astype(jnp.float32)
                turned[g, b, h * BQ : (h + 1) * BQ, :] = (rotate(field) * factor).astype(jnp.bfloat16)
            field = own[0, rows, g * HD : (g + 1) * HD].astype(jnp.float32)
            own_keys[g, b] = rotate(field).astype(jnp.bfloat16)

    def scores_of(keys, g, b, r):
        return lax.dot_general(
            keys,
            turned[g, b, r : r + TILE, :],
            (((1,), (1,)), ((), ())),
            preferred_element_type=jnp.float32,
        )

    def with_ones(values):
        return jnp.concatenate([values.T, jnp.ones((ONES, values.shape[0]), jnp.bfloat16)], axis=0)

    def weigh(values, weights):
        return lax.dot_general(
            values, weights, (((1,), (0,)), ((), ())), preferred_element_type=jnp.float32
        )

    for g in range(2):
        for b in range(BR_DEV):
            keys = own_keys[g, b]
            values = with_ones(own[1, pl.ds(pl.multiple_of(order[b] * BQ, BQ), BQ), g * HD : (g + 1) * HD])
            for r in range(0, COLS, TILE):
                scores = scores_of(keys, g, b, r)
                key_at = lax.broadcasted_iota(jnp.int32, (BQ, TILE), 0)
                token = lax.rem(lax.broadcasted_iota(jnp.int32, (BQ, TILE), 1), BQ)
                scores = jnp.where(key_at <= token, scores, NEG)
                peak = jnp.max(scores, axis=0, keepdims=True)
                weights = jnp.exp2(scores - peak).astype(jnp.bfloat16)
                mixed = weigh(values, weights)
                peaks[g, b, 0:1, r : r + TILE] = peak
                totals[g, b, 0:1, r : r + TILE] = mixed[HD : HD + 1]
                acc[g, b, :, r : r + TILE] = mixed[:HD]

    def attend(g, slot, branches=range(BR_DEV)):
        tiles = [(b, r) for b in branches for r in range(0, COLS, TILE)]
        keys = kbuf[g, slot]
        values = with_ones(vbuf[g, slot])
        on = [live[b, slot] > 0 for b in range(BR_DEV)]

        def soften(b, r, scores):
            before_peak = peaks[g, b, 0:1, r : r + TILE]
            peak = jnp.maximum(before_peak, jnp.where(on[b], jnp.max(scores, axis=0, keepdims=True), NEG))
            peaks[g, b, 0:1, r : r + TILE] = peak
            shift = jnp.where(on[b], peak, -NEG)
            weights = jnp.exp2(scores - shift).astype(jnp.bfloat16)
            return weights, jnp.exp2(before_peak - peak)

        def add(b, r, weights, fade):
            mixed = weigh(values, weights)
            acc[g, b, :, r : r + TILE] = acc[g, b, :, r : r + TILE] * fade + mixed[:HD]
            totals[g, b, 0:1, r : r + TILE] = totals[g, b, 0:1, r : r + TILE] * fade + mixed[HD : HD + 1]

        ready = [scores_of(keys, g, *tile) for tile in tiles[:AHEAD]]
        waiting = []
        for at, tile in enumerate(tiles):
            if at + AHEAD < len(tiles):
                ready.append(scores_of(keys, g, *tiles[at + AHEAD]))
            waiting.append(tile + soften(*tile, ready[at]))
            ready[at] = None
            if len(waiting) > LAG:
                add(*waiting.pop(0))
        for item in waiting:
            add(*item)

    def finish(g, b):
        for h in range(GROUP):
            span = slice(h * BQ, (h + 1) * BQ)
            mixed = acc[g, b, :, span] / totals[g, b, 0:1, span]
            obuf[b * BQ : (b + 1) * BQ, (g * GROUP + h) * HD : (g * GROUP + h + 1) * HD] = mixed.T.astype(
                jnp.bfloat16
            )

    part = BR_DEV * BQ // heads

    def out_copy(g, b, j):
        device = order[b] * 2 + j
        at = lax.rem(device - head + heads, heads) - 1
        return pltpu.make_async_remote_copy(
            src_ref=obuf.at[pl.ds(b * BQ + j * part, part), pl.ds(g * COLS, COLS)],
            dst_ref=out.at[:, pl.ds(pl.multiple_of((head * 2 + g) * COLS, COLS), COLS)],
            send_sem=out_send.at[g, at],
            recv_sem=out_recv.at[g, at],
            device_id=(node, device),
            device_id_type=MESH,
        )

    core = lax.rem(head, 2)

    def out_keep(g):
        return pltpu.make_async_copy(
            obuf.at[pl.ds(pl.multiple_of(BQ + core * part, part), part), pl.ds(g * COLS, COLS)],
            out.at[:, pl.ds(pl.multiple_of((head * 2 + g) * COLS, COLS), COLS)],
            out_local.at[g],
        )

    def exchange(g, b):
        if b == 0:
            for j in range(2):
                out_copy(g, 0, j).start()
        else:
            out_copy(g, 1, 1 - core).start()
            out_keep(g).start()

    for g in range(2):
        for copy in local_shared(g):
            copy.wait()

    def serve_at(i, steps):
        for step in steps:
            if any(plan[step + 2] for plan in plans.values()):

                @pl.when(i == step)
                def _():
                    serve(step + 2)

    def pick(i, values):
        result = jnp.int32(values[0])
        for at, value in enumerate(values[1:]):
            result = jnp.where(i == at + 1, value, result)
        return result

    first = 6 + REMOTE

    def first_step(i, carry):
        serve_at(i, range(first))
        attend(pick(i, [g for g, _ in blocks[:first]]), pick(i, [slot for _, slot in blocks[:first]]))
        return carry

    lax.fori_loop(0, first, first_step, 0)
    for b in range(BR_DEV):
        finish(0, b)
        exchange(0, b)

    last = len(blocks) - 1

    def second_step(i, carry):
        serve_at(i + first, range(first, last))
        attend(1, pick(i, SECOND_ORDER[:-1]))
        return carry

    lax.fori_loop(0, last - first, second_step, 0)
    serve(last + 2)
    for b in range(BR_DEV):
        attend(1, SECOND_ORDER[-1], (b,))
        finish(1, b)
        exchange(1, b)

    for g in range(2):
        for piece in range(PIECES):
            for blk in range(2):
                for kv in range(2):
                    up_copy(g, kv, blk, piece).wait_send()
                    down_copy(g, kv, blk, piece).wait_send()
                relay_up(g, blk, piece).wait_send()
                relay_down(g, blk, piece).wait_send()
            for kv in range(2):
                z_copy(g, kv, 1, piece).wait_send()

                @pl.when(y > 0)
                def _():
                    z_copy(g, kv, 0, piece).wait_send()

        for j in range(2):
            out_copy(g, 0, j).wait()
        out_copy(g, 1, 1 - core).wait()
        out_keep(g).wait()


def inverse_frequencies():
    half = HD // 2
    inverse = np.power(np.float64(BASE), -np.arange(half) * (2.0 / HD)).astype(np.float32)
    return np.concatenate([inverse, inverse])[None, :]


def per_device(queries, own_cache, tree_cache, shared_cache, parent, leaf):
    nodes = lax.axis_size("node")
    heads = lax.axis_size("head")
    rows = queries.shape[0]
    dma = pltpu.SemaphoreType.DMA
    anywhere = pl.BlockSpec(memory_space=pl.ANY)

    def kernel(*refs):
        attention_kernel(nodes, *refs)

    return pl.pallas_call(
        kernel,
        out_shape=jax.ShapeDtypeStruct((rows // heads, queries.shape[1] * heads), jnp.bfloat16),
        in_specs=[anywhere] * 7,
        out_specs=anywhere,
        scratch_shapes=[
            pltpu.VMEM(queries.shape, jnp.bfloat16),
            pltpu.VMEM((2, BR_DEV, COLS, HD), jnp.bfloat16),
            pltpu.VMEM(own_cache.shape, jnp.bfloat16),
            pltpu.VMEM((2, BR_DEV, BQ, HD), jnp.bfloat16),
            pltpu.VMEM((2, SLOTS, BT, HD), jnp.bfloat16),
            pltpu.VMEM((2, SLOTS, BT, HD), jnp.bfloat16),
            pltpu.VMEM((2, BR_DEV, 8, COLS), jnp.float32),
            pltpu.VMEM((2, BR_DEV, 8, COLS), jnp.float32),
            pltpu.VMEM((2, BR_DEV, HD, COLS), jnp.float32),
            pltpu.VMEM(queries.shape, jnp.bfloat16),
            pltpu.SMEM(parent.shape, jnp.int32),
            pltpu.SMEM(leaf.shape, jnp.int32),
            pltpu.VMEM((1, HD), jnp.float32),
            pltpu.SMEM((BR_DEV, 16), jnp.int32),
            dma((3,)),
            pltpu.SemaphoreType.REGULAR,
            dma,
            dma,
            dma((2, 3)),
            dma((2, 3)),
            dma((2, 2, 2, PIECES)),
            dma((2, 2, 2, PIECES)),
            dma((2, 2, 2, PIECES)),
            dma((2, 2, PIECES)),
            dma((2, 2, PIECES)),
            dma((2, SLOTS, PIECES)),
            dma((2, SLOTS, PIECES)),
            dma((2, 3)),
            dma((2, 3)),
            dma((2,)),
        ],
        compiler_params=pltpu.CompilerParams(
            collective_id=0, has_side_effects=True, vmem_limit_bytes=64 * 1024 * 1024 - 64 * 1024
        ),
        name="branch_attention",
    )(parent, leaf, jnp.asarray(inverse_frequencies()), queries, own_cache, tree_cache, shared_cache)


def solution(mesh):
    in_specs = (
        P("node", "head"),
        P(None, "node", "head"),
        P(None, "node", "head"),
        P(None, None, "head"),
        P(),
        P("node"),
    )
    out_specs = P(("node", "head"), None)
    return jax.shard_map(
        per_device, mesh=mesh, in_specs=in_specs, out_specs=out_specs, check_vma=False
    )
```

```python
import math

import jax
import jax.numpy as jnp
import numpy as np
from jax import lax
from jax.experimental import pallas as pl
from jax.experimental.pallas import tpu as pltpu
from jax.sharding import PartitionSpec as P

HD = 128
BT = 512
BQ = 128
SUB = 8
BLK_DEV = 2
BR_DEV = 2
RING = 4
GROUP = 8
COLS = GROUP * BQ
TILE = 256
AHEAD = 2
LAG = 1
ONES = 16
PIECES = 1

BASE = 1000000.0
NEG = -1e30
MESH = pl.DeviceIdType.MESH

SHARED = 2
FAR = (10, 3)
NEXT = (5, 4)
THIRD = (9, 6)
SECOND = (8, 7)
SLOTS = 11
FIRST = 3
REMOTE = 7
BACK = {0: 0, 1: -1, 3: 7, 4: 1, 5: 2, 6: 5, 9: 6, 7: 3, 8: 4}

PLAN = {
    0: (
        (0, (("far", 1, 1, 1),)),
        (1, (("up", 1, 1, 0), ("down", 0, 1, 1), ("down", 1, 0, 1), ("up", 0, 0, 1), ("up", 0, 1, 1),)),
        (2, (("far", 1, 0, 1),)),
        (3, (("down", 0, 0, 0), ("far", 0, 1, 1),)),
        (4, (("up", 1, 0, 1), ("up", 0, 1, 0), ("up", 1, 0, 0),)),
        (5, (("down", 0, 0, 1),)),
        (6, (("far", 0, 0, 1), ("down", 0, 1, 0), ("up", 0, 0, 0),)),
        (9, (("down", 1, 1, 0),)),
        (11, (("down", 1, 1, 1),)),
        (12, (("up", 1, 1, 1),)),
        (13, (("values", 1, 1), ("down", 1, 0, 0), ("keys", 0, 0),)),
        (14, (("values", 0, 1),)),
        (15, (("values", 1, 0),)),
        (17, (("keys", 1, 0), ("keys", 1, 1),)),
        (18, (("values", 0, 0),)),
        (19, (("keys", 0, 1),)),
    ),
    1: (
        (0, (("far", 0, 1, 1), ("far", 0, 0, 0),)),
        (1, (("up", 0, 0, 1), ("up", 1, 1, 0),)),
        (3, (("far", 0, 1, 0), ("on", 0, 1, 1), ("up", 0, 1, 1),)),
        (4, (("on", 0, 0, 0), ("up", 0, 0, 0), ("far", 0, 0, 1), ("far", 1, 1, 0),)),
        (5, (("up", 0, 1, 0), ("on", 0, 1, 0),)),
        (6, (("values", 0, 1),)),
        (7, (("far", 1, 1, 1), ("far", 1, 0, 0), ("up", 1, 0, 1),)),
        (9, (("far", 1, 0, 1),)),
        (11, (("keys", 0, 1),)),
        (12, (("on", 1, 1, 1), ("on", 1, 1, 0), ("keys", 1, 1),)),
        (14, (("up", 1, 0, 0), ("on", 1, 0, 0), ("up", 1, 1, 1), ("values", 0, 0), ("on", 0, 0, 1),)),
        (17, (("values", 1, 1),)),
        (18, (("keys", 1, 0),)),
        (19, (("values", 1, 0),)),
        (20, (("on", 1, 0, 1), ("keys", 0, 0),)),
    ),
    3: (
        (0, (("far", 0, 1, 1), ("far", 0, 0, 1),)),
        (2, (("values", 0, 1), ("far", 0, 1, 0),)),
        (3, (("on", 0, 1, 1),)),
        (4, (("far", 0, 0, 0),)),
        (5, (("on", 0, 0, 1), ("keys", 0, 1),)),
        (6, (("far", 1, 0, 0),)),
        (7, (("on", 0, 1, 0),)),
        (9, (("far", 1, 1, 0),)),
        (10, (("on", 0, 0, 0),)),
        (12, (("far", 1, 0, 1), ("on", 1, 0, 0), ("far", 1, 1, 1), ("on", 1, 1, 0),)),
        (14, (("on", 1, 0, 1), ("keys", 1, 1),)),
        (16, (("values", 1, 1),)),
        (18, (("values", 0, 0), ("on", 1, 1, 1),)),
        (20, (("keys", 1, 0),)),
        (21, (("keys", 0, 0), ("values", 1, 0),)),
    ),
}
FIRST_ORDER = (4, 3, 9, 5, 6, 8, 7)
SECOND_ORDER = (3, 5, 9, 6, 4, 7, 8)


def planned_steps(place, blocks):
    waited, sent = set(), set()
    steps = [[] for _ in range(len(blocks) + 2)]

    def wait(actions, *key):
        if key not in waited:
            waited.add(key)
            actions.append(("wait",) + key)

    def send(actions, op, g, *rest):
        if (op, g) + rest in sent:
            return
        if op == "values" and not any(other[0] == "values" for other in sent):
            actions.append(("ready", g))
        sent.add((op, g) + rest)
        for piece in range(PIECES):
            if op == "on":
                kv, blk = rest
                wait(actions, g, kv, FAR[blk], piece)
                actions.append(("down", g, kv, blk, piece))
                if place == 3:
                    actions.append(("up", g, kv, blk, piece))
            else:
                if op == "keys":
                    wait(actions, g, 0, NEXT[rest[0]], piece)
                elif op == "values":
                    wait(actions, g, 1, THIRD[rest[0]], piece)
                actions.append((op, g) + rest + (piece,))

    early = {step: ops for step, ops in PLAN[place]}
    for step, actions in enumerate(steps):
        for op in early.get(step, ()):
            send(actions, *op)
        if step < 2:
            continue
        if step == len(steps) - 1:
            for ops in early.values():
                for op in ops:
                    send(actions, *op)
        g, slot = blocks[step - 2]
        for blk in range(2):
            if slot == FAR[blk] and place != 0:
                send(actions, "on", g, 0, blk)
                send(actions, "on", g, 1, blk)
            if slot == NEXT[blk]:
                send(actions, "keys", g, blk)
            if slot == THIRD[blk]:
                send(actions, "values", g, blk)
        if slot >= FIRST:
            for kv in range(2):
                for piece in range(PIECES):
                    wait(actions, g, kv, slot, piece)
    return steps


def attention_kernel(
    nodes,
    parent_in,
    leaf_in,
    inverse_in,
    queries,
    own_cache,
    tree_cache,
    shared_cache,
    out,
    raw,
    turned,
    own,
    own_keys,
    kbuf,
    vbuf,
    peaks,
    totals,
    acc,
    obuf,
    parent,
    leaf,
    inverse,
    live,
    small_sem,
    ready_sem,
    load_sem,
    own_sem,
    local_k,
    local_v,
    z_send,
    up_send,
    down_send,
    relay_up_send,
    relay_down_send,
    recv_k,
    recv_v,
    out_send,
    out_recv,
    out_local,
):
    node = lax.axis_index("node")
    head = lax.axis_index("head")
    heads = 4
    y = lax.rem(node, RING)
    plane = node - y
    up = plane + lax.rem(y + 1, RING)
    down = plane + lax.rem(y + RING - 1, RING)
    after = lax.rem(node + 1, nodes)
    before = lax.rem(node + nodes - 1, nodes)
    ahead = lax.rem(node + RING, nodes)
    behind = lax.rem(node + nodes - RING, nodes)
    others = [lax.rem(head + k, heads) for k in range(1, heads)]

    barrier = pltpu.get_barrier_semaphore()
    for source in (down, up, behind, before):
        pl.semaphore_signal(barrier, inc=1, device_id=(source, head), device_id_type=MESH)
    for other in others:
        pl.semaphore_signal(barrier, inc=1, device_id=(node, other), device_id_type=MESH)

    def local_tree(g, blk):
        rows = pl.ds(blk * BT, BT)
        columns = pl.ds(g * HD, HD)
        return (
            pltpu.make_async_copy(tree_cache.at[0, rows, columns], kbuf.at[g, blk], local_k.at[g, blk]),
            pltpu.make_async_copy(tree_cache.at[1, rows, columns], vbuf.at[g, blk], local_v.at[g, blk]),
        )

    def local_shared(g):
        columns = pl.ds(g * HD, HD)
        return (
            pltpu.make_async_copy(shared_cache.at[0, :, columns], kbuf.at[g, SHARED], local_k.at[g, SHARED]),
            pltpu.make_async_copy(shared_cache.at[1, :, columns], vbuf.at[g, SHARED], local_v.at[g, SHARED]),
        )

    load_queries = pltpu.make_async_copy(queries, raw, load_sem)
    load_own = pltpu.make_async_copy(own_cache, own, own_sem)
    for g in range(2):
        for blk in range(2):
            for copy in local_tree(g, blk):
                copy.start()
    small = [
        pltpu.make_async_copy(parent_in, parent, small_sem.at[0]),
        pltpu.make_async_copy(leaf_in, leaf, small_sem.at[1]),
        pltpu.make_async_copy(inverse_in, inverse, small_sem.at[2]),
    ]
    for copy in small:
        copy.start()
    load_queries.start()
    load_own.start()
    for g in range(2):
        for copy in local_shared(g):
            copy.start()

    pl.semaphore_wait(barrier, 7)
    pl.semaphore_signal(ready_sem, inc=1, device_id=(after, head), device_id_type=MESH)

    bufs = (kbuf, vbuf)
    recvs = (recv_k, recv_v)

    def rows_of(piece):
        return pl.ds(piece * (BT // PIECES), BT // PIECES)

    def remote(kv, g, source, target, piece, sem, device):
        return pltpu.make_async_remote_copy(
            src_ref=bufs[kv].at[g, source, rows_of(piece)],
            dst_ref=bufs[kv].at[g, target, rows_of(piece)],
            send_sem=sem,
            recv_sem=recvs[kv].at[g, target, piece],
            device_id=(device, head),
            device_id_type=MESH,
        )

    passes_up = y == RING - 1
    passes_down = y > 0

    def z_copy(g, kv, blk, piece):
        rows = pl.ds(blk * BT + piece * (BT // PIECES), BT // PIECES)
        return pltpu.make_async_remote_copy(
            src_ref=tree_cache.at[kv, rows, pl.ds(g * HD, HD)],
            dst_ref=bufs[kv].at[g, FAR[blk], rows_of(piece)],
            send_sem=z_send.at[g, kv, blk, piece],
            recv_sem=recvs[kv].at[g, FAR[blk], piece],
            device_id=(ahead, head),
            device_id_type=MESH,
        )

    def up_copy(g, kv, blk, piece):
        source = jnp.where(passes_up, FAR[blk], blk)
        return remote(kv, g, source, NEXT[blk], piece, up_send.at[g, kv, blk, piece], up)

    def down_copy(g, kv, blk, piece):
        source = jnp.where(passes_down, FAR[blk], blk)
        return remote(kv, g, source, THIRD[blk], piece, down_send.at[g, kv, blk, piece], down)

    def relay_up(g, blk, piece):
        return remote(0, g, NEXT[blk], SECOND[blk], piece, relay_up_send.at[g, blk, piece], after)

    def relay_down(g, blk, piece):
        return remote(1, g, THIRD[blk], SECOND[blk], piece, relay_down_send.at[g, blk, piece], before)

    def arrived(g, kv, slot, piece):
        here = bufs[kv].at[g, slot, rows_of(piece)]
        pltpu.make_async_copy(here, here, recvs[kv].at[g, slot, piece]).wait()

    def act(op, g, *rest):
        if op == "wait":
            arrived(g, *rest)
        elif op == "far":
            z_copy(g, *rest).start()
        elif op == "up":
            up_copy(g, *rest).start()
        elif op == "down":
            down_copy(g, *rest).start()
        elif op == "keys":
            relay_up(g, *rest).start()
        elif op == "values":
            relay_down(g, *rest).start()
        else:
            pl.semaphore_wait(ready_sem, 1)

    blocks = [(g, slot) for g in range(2) for slot in range(3)]
    blocks += [(0, slot) for slot in FIRST_ORDER] + [(1, slot) for slot in SECOND_ORDER]
    plans = {place: planned_steps(place, blocks) for place in PLAN}
    at_place = {0: y == 0, 1: (y == 1) | (y == 2), 3: y == 3}

    def serve(step):
        for place, plan in plans.items():
            if plan[step]:

                @pl.when(at_place[place])
                def _():
                    for action in plan[step]:
                        act(*action)

    serve(0)
    for g in range(2):
        for blk in range(2):
            for copy in local_tree(g, blk):
                copy.wait()
    serve(1)

    for copy in small:
        copy.wait()

    order = [1 - head // 2, head // 2]

    ids = {slot: lax.rem(node * BLK_DEV + nodes * BLK_DEV - back, nodes * BLK_DEV) for slot, back in BACK.items()}
    depths = []
    for b in range(BR_DEV):
        current = leaf[order[b]]
        depth = jnp.int32(0)
        hits = {slot: jnp.int32(0) for slot in ids}
        for step in range(SUB):
            valid = current >= 0
            depth = depth + valid.astype(jnp.int32)
            for slot, block in ids.items():
                hits[slot] = hits[slot] + (current == block).astype(jnp.int32)
            current = jnp.where(valid, parent[jnp.maximum(current, 0)], -1)
        depths.append(depth)
        for slot in ids:
            live[b, slot] = hits[slot]
        live[b, SHARED] = jnp.int32(1)

    load_queries.wait()
    load_own.wait()
    offsets = lax.broadcasted_iota(jnp.int32, (BQ, HD), 0)
    lane = lax.broadcasted_iota(jnp.int32, (BQ, HD), 1)
    factor = math.log2(math.e) / math.sqrt(HD)
    for b in range(BR_DEV):
        position = BT * (depths[b] + 1) + offsets
        angle = position.astype(jnp.float32) * inverse[...]
        cosine = jnp.cos(angle)
        sine = jnp.sin(angle)
        sine = jnp.where(lane < HD // 2, -sine, sine)

        def rotate(field):
            return field * cosine + pltpu.roll(field, HD // 2, 1) * sine

        rows = pl.ds(pl.multiple_of(order[b] * BQ, BQ), BQ)
        for g in range(2):
            for h in range(GROUP):
                field = raw[rows, (g * GROUP + h) * HD : (g * GROUP + h + 1) * HD].astype(jnp.float32)
                turned[g, b, h * BQ : (h + 1) * BQ, :] = (rotate(field) * factor).astype(jnp.bfloat16)
            field = own[0, rows, g * HD : (g + 1) * HD].astype(jnp.float32)
            own_keys[g, b] = rotate(field).astype(jnp.bfloat16)

    def scores_of(keys, g, b, r):
        return lax.dot_general(
            keys,
            turned[g, b, r : r + TILE, :],
            (((1,), (1,)), ((), ())),
            preferred_element_type=jnp.float32,
        )

    def with_ones(values):
        return jnp.concatenate([values.T, jnp.ones((ONES, values.shape[0]), jnp.bfloat16)], axis=0)

    def weigh(values, weights):
        return lax.dot_general(
            values, weights, (((1,), (0,)), ((), ())), preferred_element_type=jnp.float32
        )

    for g in range(2):
        for b in range(BR_DEV):
            keys = own_keys[g, b]
            values = with_ones(own[1, pl.ds(pl.multiple_of(order[b] * BQ, BQ), BQ), g * HD : (g + 1) * HD])
            for r in range(0, COLS, TILE):
                scores = scores_of(keys, g, b, r)
                key_at = lax.broadcasted_iota(jnp.int32, (BQ, TILE), 0)
                token = lax.rem(lax.broadcasted_iota(jnp.int32, (BQ, TILE), 1), BQ)
                scores = jnp.where(key_at <= token, scores, NEG)
                peak = jnp.max(scores, axis=0, keepdims=True)
                weights = jnp.exp2(scores - peak).astype(jnp.bfloat16)
                mixed = weigh(values, weights)
                peaks[g, b, 0:1, r : r + TILE] = peak
                totals[g, b, 0:1, r : r + TILE] = mixed[HD : HD + 1]
                acc[g, b, :, r : r + TILE] = mixed[:HD]

    def attend(g, slot, branches=range(BR_DEV)):
        tiles = [(b, r) for b in branches for r in range(0, COLS, TILE)]
        keys = kbuf[g, slot]
        values = with_ones(vbuf[g, slot])
        on = [live[b, slot] > 0 for b in range(BR_DEV)]

        def soften(b, r, scores):
            before_peak = peaks[g, b, 0:1, r : r + TILE]
            peak = jnp.maximum(before_peak, jnp.where(on[b], jnp.max(scores, axis=0, keepdims=True), NEG))
            peaks[g, b, 0:1, r : r + TILE] = peak
            shift = jnp.where(on[b], peak, -NEG)
            weights = jnp.exp2(scores - shift).astype(jnp.bfloat16)
            return weights, jnp.exp2(before_peak - peak)

        def add(b, r, weights, fade):
            mixed = weigh(values, weights)
            acc[g, b, :, r : r + TILE] = acc[g, b, :, r : r + TILE] * fade + mixed[:HD]
            totals[g, b, 0:1, r : r + TILE] = totals[g, b, 0:1, r : r + TILE] * fade + mixed[HD : HD + 1]

        ready = [scores_of(keys, g, *tile) for tile in tiles[:AHEAD]]
        waiting = []
        for at, tile in enumerate(tiles):
            if at + AHEAD < len(tiles):
                ready.append(scores_of(keys, g, *tiles[at + AHEAD]))
            waiting.append(tile + soften(*tile, ready[at]))
            ready[at] = None
            if len(waiting) > LAG:
                add(*waiting.pop(0))
        for item in waiting:
            add(*item)

    def finish(g, b):
        for h in range(GROUP):
            span = slice(h * BQ, (h + 1) * BQ)
            mixed = acc[g, b, :, span] / totals[g, b, 0:1, span]
            obuf[b * BQ : (b + 1) * BQ, (g * GROUP + h) * HD : (g * GROUP + h + 1) * HD] = mixed.T.astype(
                jnp.bfloat16
            )

    part = BR_DEV * BQ // heads

    def out_copy(g, b, j):
        device = order[b] * 2 + j
        at = lax.rem(device - head + heads, heads) - 1
        return pltpu.make_async_remote_copy(
            src_ref=obuf.at[pl.ds(b * BQ + j * part, part), pl.ds(g * COLS, COLS)],
            dst_ref=out.at[:, pl.ds(pl.multiple_of((head * 2 + g) * COLS, COLS), COLS)],
            send_sem=out_send.at[g, at],
            recv_sem=out_recv.at[g, at],
            device_id=(node, device),
            device_id_type=MESH,
        )

    core = lax.rem(head, 2)

    def out_keep(g):
        return pltpu.make_async_copy(
            obuf.at[pl.ds(pl.multiple_of(BQ + core * part, part), part), pl.ds(g * COLS, COLS)],
            out.at[:, pl.ds(pl.multiple_of((head * 2 + g) * COLS, COLS), COLS)],
            out_local.at[g],
        )

    def exchange(g, b):
        if b == 0:
            for j in range(2):
                out_copy(g, 0, j).start()
        else:
            out_copy(g, 1, 1 - core).start()
            out_keep(g).start()

    for g in range(2):
        for copy in local_shared(g):
            copy.wait()

    def serve_at(i, steps):
        for step in steps:
            if any(plan[step + 2] for plan in plans.values()):

                @pl.when(i == step)
                def _():
                    serve(step + 2)

    def pick(i, values):
        result = jnp.int32(values[0])
        for at, value in enumerate(values[1:]):
            result = jnp.where(i == at + 1, value, result)
        return result

    first = 6 + REMOTE

    def first_step(i, carry):
        serve_at(i, range(first))
        attend(pick(i, [g for g, _ in blocks[:first]]), pick(i, [slot for _, slot in blocks[:first]]))
        return carry

    lax.fori_loop(0, first, first_step, 0)
    serve(first + 2)
    for b in range(BR_DEV):
        finish(0, b)
        exchange(0, b)

    last = len(blocks) - 1

    def second_step(i, carry):
        serve_at(i + first, range(first + 1, last))
        attend(1, pick(i, SECOND_ORDER[:-1]))
        return carry

    lax.fori_loop(0, last - first, second_step, 0)
    serve(last + 2)
    for b in range(BR_DEV):
        attend(1, SECOND_ORDER[-1], (b,))
        finish(1, b)
        exchange(1, b)

    for g in range(2):
        for piece in range(PIECES):
            for blk in range(2):
                for kv in range(2):
                    up_copy(g, kv, blk, piece).wait_send()
                    down_copy(g, kv, blk, piece).wait_send()
                relay_up(g, blk, piece).wait_send()
                relay_down(g, blk, piece).wait_send()
            for kv in range(2):
                z_copy(g, kv, 1, piece).wait_send()

                @pl.when(y > 0)
                def _():
                    z_copy(g, kv, 0, piece).wait_send()

        for j in range(2):
            out_copy(g, 0, j).wait()
        out_copy(g, 1, 1 - core).wait()
        out_keep(g).wait()


def inverse_frequencies():
    half = HD // 2
    inverse = np.power(np.float64(BASE), -np.arange(half) * (2.0 / HD)).astype(np.float32)
    return np.concatenate([inverse, inverse])[None, :]


def per_device(queries, own_cache, tree_cache, shared_cache, parent, leaf):
    nodes = lax.axis_size("node")
    heads = lax.axis_size("head")
    rows = queries.shape[0]
    dma = pltpu.SemaphoreType.DMA
    anywhere = pl.BlockSpec(memory_space=pl.ANY)

    def kernel(*refs):
        attention_kernel(nodes, *refs)

    return pl.pallas_call(
        kernel,
        out_shape=jax.ShapeDtypeStruct((rows // heads, queries.shape[1] * heads), jnp.bfloat16),
        in_specs=[anywhere] * 7,
        out_specs=anywhere,
        scratch_shapes=[
            pltpu.VMEM(queries.shape, jnp.bfloat16),
            pltpu.VMEM((2, BR_DEV, COLS, HD), jnp.bfloat16),
            pltpu.VMEM(own_cache.shape, jnp.bfloat16),
            pltpu.VMEM((2, BR_DEV, BQ, HD), jnp.bfloat16),
            pltpu.VMEM((2, SLOTS, BT, HD), jnp.bfloat16),
            pltpu.VMEM((2, SLOTS, BT, HD), jnp.bfloat16),
            pltpu.VMEM((2, BR_DEV, 8, COLS), jnp.float32),
            pltpu.VMEM((2, BR_DEV, 8, COLS), jnp.float32),
            pltpu.VMEM((2, BR_DEV, HD, COLS), jnp.float32),
            pltpu.VMEM(queries.shape, jnp.bfloat16),
            pltpu.SMEM(parent.shape, jnp.int32),
            pltpu.SMEM(leaf.shape, jnp.int32),
            pltpu.VMEM((1, HD), jnp.float32),
            pltpu.SMEM((BR_DEV, 16), jnp.int32),
            dma((3,)),
            pltpu.SemaphoreType.REGULAR,
            dma,
            dma,
            dma((2, 3)),
            dma((2, 3)),
            dma((2, 2, 2, PIECES)),
            dma((2, 2, 2, PIECES)),
            dma((2, 2, 2, PIECES)),
            dma((2, 2, PIECES)),
            dma((2, 2, PIECES)),
            dma((2, SLOTS, PIECES)),
            dma((2, SLOTS, PIECES)),
            dma((2, 3)),
            dma((2, 3)),
            dma((2,)),
        ],
        compiler_params=pltpu.CompilerParams(
            collective_id=0, has_side_effects=True, vmem_limit_bytes=64 * 1024 * 1024 - 64 * 1024
        ),
        name="branch_attention",
    )(parent, leaf, jnp.asarray(inverse_frequencies()), queries, own_cache, tree_cache, shared_cache)


def solution(mesh):
    in_specs = (
        P("node", "head"),
        P(None, "node", "head"),
        P(None, "node", "head"),
        P(None, None, "head"),
        P(),
        P("node"),
    )
    out_specs = P(("node", "head"), None)
    return jax.shard_map(
        per_device, mesh=mesh, in_specs=in_specs, out_specs=out_specs, check_vma=False
    )
```
